128 devices in a mesh: rep: 32 (over x, y, core), opt: 4 (over z).
Axes of the slice: x: 4, y: 4, z: 4, core: 2. Of those that a mesh axis runs over, the one named last changes fastest.
Arguments:
- context: bfloat16 [131072, 1024], P(('rep', 'opt')), may hold values from -12 to 12
- residual_in: bfloat16 [131072, 1024], P(('rep', 'opt')), may hold values from -6 to 6
- cotangent: bfloat16 [131072, 1024], P(('rep', 'opt')), may hold values from -6 to 6
- weight: bfloat16 [1024, 1024], replicated, may hold values from -0.1875 to 0.1875
- master: float32 [1024, 1024], P('opt'), may hold values from -1.875 to 1.875
- moment_first: float32 [1024, 1024], P('opt'), may hold values from -0.004 to 0.004
- moment_second: float32 [1024, 1024], P('opt'), may hold values from 1e-07 to 1e-05
- out_bias: float32 [1024], replicated, may hold values from -4 to 4
- ln_gain: float32 [1024], replicated, may hold values from 0.5 to 1.5
- ln_shift: float32 [1024], replicated, may hold values from -4 to 4
- vector_first: float32 [3, 1024], replicated, may hold values from -0.015625 to 0.015625
- vector_second: float32 [3, 1024], replicated, may hold values from 1e-07 to 1e-05
Outputs:
- d_context: bfloat16 [131072, 1024], P(('rep', 'opt'))
- d_resid: bfloat16 [131072, 1024], P(('rep', 'opt'))
- new_weight: bfloat16 [1024, 1024], replicated
- new_master: float32 [1024, 1024], P('opt')
- new_first: float32 [1024, 1024], P('opt')
- new_second: float32 [1024, 1024], P('opt')
- new_vectors: float32 [3, 1024], replicated
- new_vector_first: float32 [3, 1024], replicated
- new_vector_second: float32 [3, 1024], replicated
The draws below stay inside these ranges and needn't reach their ends.
All inputs are finite; a program needn't handle non-finite values.
Results may differ from the reference program's by a relative error of at most 0.0085.
Values may be sent and summed in bfloat16 or wider, within the bound.
No kernel may reach another device: no remote copies, remote signals or barrier semaphores. Data moves between devices by JAX's collectives and lax.ppermute only.
A program may use at most 128 MiB of HBM per device.

```python
import math
import jax
import jax.numpy as jnp
from jax import lax

D = 1024
TOKENS = 131072


def row_profile(top):
    position = jnp.arange(D, dtype=jnp.float32) / (D - 1.0)
    return jnp.exp(jnp.log(top) * (position - 0.5)).reshape(D, 1)


def scaled_field(key, top, spread):
    values = jnp.clip(jax.random.normal(key, (D, D), jnp.float32), -6.0, 6.0)
    profile = row_profile(top)
    return values * profile * spread


def draw_master(key, part):
    key = jax.random.fold_in(key, 11)
    return scaled_field(key, 6.0, D ** (-0.5)).astype(jnp.float32)


def draw_moment_first(key, part):
    key = jax.random.fold_in(key, 23)
    return scaled_field(key, 6.0, 0.0002).astype(jnp.float32)


def draw_context(key, part):
    key = jax.random.fold_in(key, 37)
    values = jnp.clip(jax.random.normal(key, (TOKENS, D), jnp.float32), -6.0, 6.0)
    profile = row_profile(4.0).reshape(1, D)
    return (values * profile).astype(jnp.bfloat16)


def steps_of(stream_key, extent, pieces, least, largest):
    gain, own = 1.0, jax.random.fold_in(stream_key, 6)
    for axis_at, shards_of in pieces:
        steps = jnp.exp(jax.random.uniform(jax.random.fold_in(own, axis_at), (shards_of,), jnp.float32, least / len(pieces), largest / len(pieces)))
        gain = gain * jnp.repeat(steps, extent[axis_at] // shards_of).reshape([-1 if axis == axis_at else 1 for axis in range(len(extent))])
    return gain


def bell_draw(stream_key, shape, width, most, split=(), held_as=jnp.bfloat16):
    entries = jax.random.normal(stream_key, shape, jnp.float32) * width
    if len(split) > 0:
        entries = steps_of(stream_key, shape, split, -0.22, 0.18) * entries
    return jnp.clip(entries, min=-most, max=most).astype(held_as)


def setup_inputs(seed: int = 0) -> dict:
    keys = jax.random.split(jax.random.key(seed), 13)
    return {
        "context": draw_context(jax.random.fold_in(keys[12], 71), 0),
        "residual_in": bell_draw(keys[1], (TOKENS, D), 1.0, 6.0, ((0, 128),)),
        "cotangent": bell_draw(keys[2], (TOKENS, D), 1.0, 6.0, ((0, 128),)),
        "weight": bell_draw(keys[3], (D, D), D ** -0.5, 0.1875),
        "master": draw_master(jax.random.fold_in(keys[12], 71), 0),
        "moment_first": draw_moment_first(jax.random.fold_in(keys[12], 71), 0),
        "moment_second": jnp.clip(jnp.exp(math.log(9.999999747378752e-06) - 4.6051701 * jax.random.uniform(keys[6], (D, D), jnp.float32) ** steps_of(keys[6], (D, D), ((0, 4),), -0.2, 0.2)), 1.0000000116860974e-07, 9.999999747378752e-06),
        "out_bias": bell_draw(keys[7], (D,), 0.5, 4.0, (), jnp.float32),
        "ln_gain": jnp.clip(1.0 + 0.1 * jax.random.normal(keys[8], (D,), jnp.float32), 0.5, 1.5),
        "ln_shift": bell_draw(keys[9], (D,), 0.5, 4.0, (), jnp.float32),
        "vector_first": bell_draw(keys[10], (3, D), 0.001, 0.015625, (), jnp.float32),
        "vector_second": jnp.clip(jnp.exp(jax.random.uniform(keys[11], (3, D), jnp.float32, math.log(1.0000000116860974e-07), math.log(9.999999747378752e-06))), 1.0000000116860974e-07, 9.999999747378752e-06),
    }


beta_one = 0.9
beta_two = 0.999
adam_eps = 1e-06
learn_rate = 0.2
decay_rate = 0.01
max_norm = 1.0

def lamb_update(param, grad, first, second, decay, axis):
    first_new = beta_one * first + (1.0 - beta_one) * grad
    second_new = beta_two * second + (1.0 - beta_two) * grad * grad
    update = first_new / (jnp.sqrt(second_new) + adam_eps) + decay * param
    weight_size = jnp.sqrt(lax.optimization_barrier(jnp.sum(param * param, axis=axis, keepdims=True)))
    update_size = jnp.sqrt(lax.optimization_barrier(jnp.sum(update * update, axis=axis, keepdims=True)) + 1e-06)
    trust = weight_size / update_size
    return (param - learn_rate * trust * update, first_new, second_new)

def reference(context, residual_in, cotangent, weight, master, moment_first, moment_second, out_bias, ln_gain, ln_shift, vector_first, vector_second):
    pre = residual_in.astype(jnp.float32) + jnp.dot(context, weight, preferred_element_type=jnp.float32) + out_bias
    centred = pre - lax.optimization_barrier(jnp.mean(pre, axis=1, keepdims=True))
    rstd = lax.rsqrt(lax.optimization_barrier(jnp.mean(centred * centred, axis=1, keepdims=True)) + 1e-05)
    normed = centred * rstd
    grad_out = cotangent.astype(jnp.float32)
    scaled = grad_out * ln_gain
    d_pre = rstd * (scaled - lax.optimization_barrier(jnp.mean(scaled, axis=1, keepdims=True)) - normed * lax.optimization_barrier(jnp.mean(scaled * normed, axis=1, keepdims=True)))
    d_resid = d_pre.astype(jnp.bfloat16)
    d_context = jnp.dot(d_resid, weight.T, preferred_element_type=jnp.float32).astype(jnp.bfloat16)
    grad_weight = jnp.dot(context.T, d_resid, preferred_element_type=jnp.float32)
    grad_vectors = jnp.stack([lax.optimization_barrier(jnp.sum(d_pre, axis=0)), lax.optimization_barrier(jnp.sum(grad_out * normed, axis=0)), lax.optimization_barrier(jnp.sum(grad_out, axis=0))])
    total = jnp.sqrt(jnp.sum(grad_weight * grad_weight) + jnp.sum(grad_vectors * grad_vectors))
    factor = 1.0 / jnp.maximum(1.0, total / max_norm)
    new_master, new_first, new_second = lamb_update(master, grad_weight * factor, moment_first, moment_second, decay_rate, None)
    vectors = jnp.stack([out_bias, ln_gain, ln_shift])
    new_vectors, new_vector_first, new_vector_second = lamb_update(vectors, grad_vectors * factor, vector_first, vector_second, 0.0, 1)
    new_weight = new_master.astype(jnp.bfloat16)
    return (d_context, d_resid, new_weight, new_master, new_first, new_second, new_vectors, new_vector_first, new_vector_second)
```

```python
import jax
import jax.numpy as jnp
from jax import lax
from jax.experimental import pallas as pl
from jax.experimental.pallas import tpu as pltpu
from jax.sharding import PartitionSpec as P

beta_one = 0.9
beta_two = 0.999
adam_eps = 1e-06
learn_rate = 0.2
decay_rate = 0.01
max_norm = 1.0

D = 1024
BLOCK = 256
F32 = jnp.float32
BF16 = jnp.bfloat16
MIB = 1024 * 1024
AXES = ("rep", "opt")
VMEM = pl.BlockSpec(memory_space=pltpu.VMEM)
SMEM = pl.BlockSpec(memory_space=pltpu.SMEM)
HOPS = (1, 3, 2)


def place(x, y, c, z):
    return (((x % 4) * 4 + y % 4) * 2 + c % 2) * 4 + z % 4


def shift(value, x=0, y=0, c=0, z=0):
    pairs = [
        (place(i, j, k, m), place(i + x, j + y, k + c, m + z))
        for i in range(4)
        for j in range(4)
        for k in range(2)
        for m in range(4)
    ]
    return lax.ppermute(value, AXES, pairs)


def call(kernel, outs, ins, specs=None, scratch=(), cost=None, limit=60, **more):
    return pl.pallas_call(
        kernel,
        out_shape=[jax.ShapeDtypeStruct(shape, dtype) for shape, dtype in outs],
        in_specs=[SMEM] + [VMEM] * (len(ins) - 1) if specs is None else specs,
        out_specs=more.pop("out_specs", [VMEM] * len(outs)),
        scratch_shapes=list(scratch),
        cost_estimate=cost,
        compiler_params=pltpu.CompilerParams(vmem_limit_bytes=limit * MIB),
        **more,
    )(*ins)


def sum_pairs(own, hop1, hop3, hop2):
    return (own.astype(F32) + hop2.astype(F32)) + (hop1.astype(F32) + hop3.astype(F32))


def split_vectors(rows):
    high = rows.astype(BF16).astype(F32)
    return jnp.concatenate([high, rows - high], axis=0).astype(BF16)


def join_vectors(message):
    wide = message.astype(F32)
    return wide[0:8] + wide[8:16]


def backward_kernel(
    at, ctx, res, cot, weight, bias, gain, dres, send, keep, ctxs, dress, pre, sums
):
    step = pl.program_id(0)
    rows = pl.ds(pl.multiple_of(step * BLOCK, BLOCK), BLOCK)
    for m in range(4):
        ctxs[m, rows, :] = ctx[:, m * 256 : (m + 1) * 256]
    pre[...] = jnp.dot(ctx[...], weight[...], preferred_element_type=F32)

    @pl.when(step == 0)
    def _():
        sums[...] = jnp.zeros_like(sums)

    bias_row = bias[...]
    gain_row = gain[...]

    def chunk(i, carry):
        at_rows = pl.ds(pl.multiple_of(i * 16, 16), 16)
        value = pre[at_rows, :] + res[at_rows, :].astype(F32) + bias_row
        grad_out = cot[at_rows, :].astype(F32)
        scaled = grad_out * gain_row
        mean = jnp.sum(value, axis=1, keepdims=True) * (1.0 / D)
        mean_scaled = jnp.sum(scaled, axis=1, keepdims=True) * (1.0 / D)
        centred = value - mean
        var = jnp.sum(centred * centred, axis=1, keepdims=True) * (1.0 / D)
        cross = jnp.sum(scaled * centred, axis=1, keepdims=True) * (1.0 / D)
        rstd = lax.rsqrt(var + 1e-05)
        normed = centred * rstd
        d_pre = rstd * (scaled - mean_scaled - normed * (cross * rstd))
        d_low = d_pre.astype(BF16)
        dres[at_rows, :] = d_low
        dress[pl.ds(pl.multiple_of(step * BLOCK + i * 16, 16), 16), :] = d_low
        moved = grad_out * normed
        sums[0] += d_pre[0:8] + d_pre[8:16]
        sums[1] += moved[0:8] + moved[8:16]
        sums[2] += grad_out[0:8] + grad_out[8:16]
        return carry

    lax.fori_loop(0, BLOCK // 16, chunk, 0, unroll=2)

    @pl.when(step == D // BLOCK - 1)
    def _():
        core = at[2]

        def rows_of(m):
            return lax.dot_general(
                ctxs[m], dress[...], (((0,), (0,)), ((), ())), preferred_element_type=F32
            ).astype(BF16)

        for half in range(2):
            send[half * 256 : (half + 1) * 256, :] = rows_of((1 - core) * 2 + half)
        for half in range(2):
            keep[half * 256 : (half + 1) * 256, :] = rows_of(core * 2 + half)
        total = [jnp.sum(sums[k], axis=0, keepdims=True) for k in range(3)]
        message = split_vectors(jnp.concatenate(total + [jnp.zeros((5, D), F32)], axis=0))
        send[512:528, :] = message
        keep[512:528, :] = message


def backward(at, context, residual_in, cotangent, weight, bias, gain):
    block = pl.BlockSpec((BLOCK, D), lambda i: (i, 0))
    whole = pl.BlockSpec((D, D), lambda i: (0, 0))
    row = pl.BlockSpec((1, D), lambda i: (0, 0))
    half = pl.BlockSpec((528, D), lambda i: (0, 0))
    return call(
        backward_kernel,
        [((D, D), BF16), ((528, D), BF16), ((528, D), BF16)],
        (at, context, residual_in, cotangent, weight, bias, gain),
        specs=[SMEM, block, block, block, whole, row, row],
        out_specs=[block, half, half],
        grid=(D // BLOCK,),
        scratch=[
            pltpu.VMEM((4, D, 256), BF16),
            pltpu.VMEM((D, D), BF16),
            pltpu.VMEM((BLOCK, D), F32),
            pltpu.VMEM((3, 8, D), F32),
        ],
        cost=pl.CostEstimate(flops=4 * D**3, bytes_accessed=14 * MIB, transcendentals=D),
        limit=40,
    )


def context_kernel(dres, weight, out):
    out[...] = lax.dot_general(
        dres[...], weight[...], (((1,), (1,)), ((), ())), preferred_element_type=F32
    ).astype(BF16)


def context_grad(d_resid, weight):
    block = pl.BlockSpec((BLOCK, D), lambda i: (i, 0))
    return call(
        context_kernel,
        [((D, D), BF16)],
        (d_resid, weight),
        specs=[block, pl.BlockSpec((D, D), lambda i: (0, 0))],
        out_specs=[block],
        grid=(D // BLOCK,),
        cost=pl.CostEstimate(flops=2 * D**3, bytes_accessed=6 * MIB, transcendentals=0),
        limit=24,
    )[0]


def pack_kernel(at, master, first, second, out):
    out[0] = master[...].astype(BF16)
    out[1] = first[...].astype(BF16)
    out[2] = second[...].astype(BF16)


def pack_state(at, master, first, second):
    return pl.pallas_call(
        pack_kernel,
        out_shape=jax.ShapeDtypeStruct((3, 128, D), BF16),
        grid_spec=pltpu.PrefetchScalarGridSpec(
            num_scalar_prefetch=1,
            grid=(1,),
            in_specs=[pl.BlockSpec((128, D), lambda i, at: (at[2], 0))] * 3,
            out_specs=pl.BlockSpec((3, 128, D), lambda i, at: (0, 0, 0)),
        ),
        compiler_params=pltpu.CompilerParams(vmem_limit_bytes=16 * MIB),
    )(at, master, first, second)


def state_kernel(at, master, first, second, *rest):
    near, other, out = rest[0:3], rest[3:6], rest[6]
    core, z = at[2], at[3]
    own = pl.ds(pl.multiple_of(z * 256, 256), 256)
    out[0, own, :] = master[...].astype(BF16)
    out[1, own, :] = first[...].astype(BF16)
    out[2, own, :] = second[...].astype(BF16)
    for hop, mine, others in zip(HOPS, near, other):
        base = lax.rem(z + 4 - hop, 4) * 256
        out[:, pl.ds(pl.multiple_of(base + core * 128, 128), 128), :] = mine[...]
        out[:, pl.ds(pl.multiple_of(base + (1 - core) * 128, 128), 128), :] = others[...]


def core_kernel(at, keep, got, *outs):
    a_outs, b_outs = outs[0:4], outs[4:8]
    x, y = at[0], at[1]
    message = split_vectors(join_vectors(keep[512:528, :]) + join_vectors(got[512:528, :]))
    for hop, out in zip((0,) + HOPS, a_outs):
        rows = pl.ds(pl.multiple_of(lax.rem(x + hop, 4) * 64, 64), 64)
        out[0:64, :] = (keep[rows, :].astype(F32) + got[rows, :].astype(F32)).astype(BF16)
        out[64:80, :] = message
    for hop, out in zip((0,) + HOPS, b_outs):
        rows = pl.ds(pl.multiple_of(256 + lax.rem(y + hop, 4) * 64, 64), 64)
        out[...] = (keep[rows, :].astype(F32) + got[rows, :].astype(F32)).astype(BF16)


def second_kernel(at, *refs):
    a_ins, b_ins, a_outs, b_outs = refs[0:4], refs[4:8], refs[8:12], refs[12:16]
    x, y = at[0], at[1]
    message = split_vectors(sum_pairs(*[join_vectors(ref[64:80, :]) for ref in a_ins]))
    for hop, out in zip((0,) + HOPS, a_outs):
        rows = pl.ds(pl.multiple_of(lax.rem(y + hop, 4) * 16, 16), 16)
        out[0:16, :] = sum_pairs(*[ref[rows, :] for ref in a_ins]).astype(BF16)
        out[16:32, :] = message
    for hop, out in zip((0,) + HOPS, b_outs):
        rows = pl.ds(pl.multiple_of(lax.rem(x + hop, 4) * 16, 16), 16)
        out[...] = sum_pairs(*[ref[rows, :] for ref in b_ins]).astype(BF16)


def third_kernel(*refs):
    a_ins, b_ins, out = refs[0:4], refs[4:8], refs[8]
    out[0:16, :] = sum_pairs(*[ref[0:16, :] for ref in a_ins]).astype(BF16)
    out[16:32, :] = sum_pairs(*[ref[...] for ref in b_ins]).astype(BF16)
    out[32:48, :] = split_vectors(sum_pairs(*[join_vectors(ref[16:32, :]) for ref in a_ins]))


def last_kernel(*refs):
    ins, (a_out, b_out, vectors) = refs[0:4], refs[4:7]
    a_out[...] = sum_pairs(*[ref[0:16, :] for ref in ins]).astype(BF16)
    b_out[...] = sum_pairs(*[ref[16:32, :] for ref in ins]).astype(BF16)
    vectors[...] = sum_pairs(*[join_vectors(ref[32:48, :]) for ref in ins])


def lines_kernel(at, *refs):
    a_ins, b_ins, a_out, b_out = refs[0:4], refs[4:8], refs[8], refs[9]
    x, y = at[0], at[1]
    for hop, mine, other in zip((0,) + HOPS, a_ins, b_ins):
        a_out[pl.ds(pl.multiple_of(lax.rem(y + 4 - hop, 4) * 16, 16), 16), :] = mine[...]
        b_out[pl.ds(pl.multiple_of(lax.rem(x + 4 - hop, 4) * 16, 16), 16), :] = other[...]


def step_of(grad, first, second, param, decay):
    first_new = beta_one * first + (1.0 - beta_one) * grad
    second_new = beta_two * second + (1.0 - beta_two) * grad * grad
    update = first_new / (jnp.sqrt(second_new) + adam_eps) + decay * param
    return first_new, second_new, update


def lamb_kernel(at, *refs):
    pieces, refs = refs[0:16], refs[16:]
    vec_grad, state, master, first, second, vectors, vec_first, vec_second = refs[0:8]
    weight_out, master_out, first_out, second_out = refs[8:12]
    vec_out, vec_first_out, vec_second_out = refs[12:15]
    grad, update = refs[15:17]
    x, y, core, z = at[0], at[1], at[2], at[3]

    for which in range(2):
        base = lax.rem(core + which, 2) * 512
        for n, hop in enumerate((0,) + HOPS):
            a_at = base + lax.rem(x + 4 - hop, 4) * 64
            b_at = base + 256 + lax.rem(y + 4 - hop, 4) * 64
            grad[pl.ds(pl.multiple_of(a_at, 64), 64), :] = pieces[which * 8 + n][...]
            grad[pl.ds(pl.multiple_of(b_at, 64), 64), :] = pieces[which * 8 + 4 + n][...]

    def fold(value):
        return value[0:8] + value[8:16]

    zero = jnp.zeros((8, D), F32)

    def square(i, total):
        g = grad[pl.ds(pl.multiple_of(i * 16, 16), 16), :].astype(F32)
        return total + fold(g * g)

    grad_sq = jnp.sum(lax.fori_loop(0, D // 16, square, zero, unroll=4))
    grad_vectors = vec_grad[0:3, :]
    total = jnp.sqrt(
        jnp.full((1, 1), grad_sq + jnp.sum(grad_vectors * grad_vectors), F32)
    )
    factor = 1.0 / jnp.maximum(1.0, total / max_norm)

    def full(i, totals):
        rows = pl.ds(pl.multiple_of(i * 16, 16), 16)
        g = grad[rows, :].astype(F32) * factor
        w = state[0, rows, :].astype(F32)
        _, _, u = step_of(
            g, state[1, rows, :].astype(F32), state[2, rows, :].astype(F32), w, decay_rate
        )
        update[rows, :] = u
        return totals[0] + fold(u * u), totals[1] + fold(w * w)

    update_sq, weight_sq = lax.fori_loop(0, D // 16, full, (zero, zero), unroll=2)
    update_sq = jnp.full((1, 1), jnp.sum(update_sq), F32)
    weight_sq = jnp.full((1, 1), jnp.sum(weight_sq), F32)
    rate = learn_rate * (jnp.sqrt(weight_sq) / jnp.sqrt(update_sq + 1e-06))

    def finish(i, carry):
        rows = pl.ds(pl.multiple_of(i * 16, 16), 16)
        weight_out[rows, :] = (state[0, rows, :].astype(F32) - rate * update[rows, :]).astype(BF16)
        return carry

    lax.fori_loop(0, D // 16, finish, 0, unroll=2)

    def shard(i, carry):
        rows = pl.ds(pl.multiple_of(i * 16, 16), 16)
        g = grad[pl.ds(pl.multiple_of(z * 256 + i * 16, 16), 16), :].astype(F32) * factor
        w = master[rows, :]
        first_new, second_new, u = step_of(g, first[rows, :], second[rows, :], w, decay_rate)
        first_out[rows, :] = first_new
        second_out[rows, :] = second_new
        master_out[rows, :] = w - rate * u
        return carry

    lax.fori_loop(0, 256 // 16, shard, 0, unroll=2)

    params = vectors[...]
    first_new, second_new, u = step_of(
        grad_vectors * factor, vec_first[...], vec_second[...], params, 0.0
    )
    trust = jnp.sqrt(jnp.sum(params * params, axis=1, keepdims=True)) / jnp.sqrt(
        jnp.sum(u * u, axis=1, keepdims=True) + 1e-06
    )
    vec_out[...] = params - learn_rate * trust * u
    vec_first_out[...] = first_new
    vec_second_out[...] = second_new


def on_device(
    context,
    residual_in,
    cotangent,
    weight,
    master,
    moment_first,
    moment_second,
    out_bias,
    ln_gain,
    ln_shift,
    vector_first,
    vector_second,
):
    rep, z = lax.axis_index("rep"), lax.axis_index("opt")
    at = jnp.stack([rep // 8, (rep // 2) % 4, rep % 2, z]).astype(jnp.int32)

    half_state = pack_state(at, master, moment_first, moment_second)
    near = [shift(half_state, z=hop) for hop in HOPS]

    d_resid, send, keep = backward(
        at,
        context,
        residual_in,
        cotangent,
        weight,
        out_bias.reshape(1, D),
        ln_gain.reshape(1, D),
    )
    got = shift(send, c=1)
    d_context = context_grad(d_resid, weight)

    outs = call(core_kernel, [((80, D), BF16)] * 4 + [((64, D), BF16)] * 4, (at, keep, got))
    a, b = outs[0:4], outs[4:8]
    a = [a[0]] + [shift(v, x=hop) for hop, v in zip(HOPS, a[1:])]
    b = [b[0]] + [shift(v, y=hop) for hop, v in zip(HOPS, b[1:])]

    outs = call(second_kernel, [((32, D), BF16)] * 4 + [((16, D), BF16)] * 4, (at, *a, *b))
    a, b = outs[0:4], outs[4:8]
    a = [a[0]] + [shift(v, y=hop) for hop, v in zip(HOPS, a[1:])]
    b = [b[0]] + [shift(v, x=hop) for hop, v in zip(HOPS, b[1:])]

    (message,) = call(third_kernel, [((48, D), BF16)], (*a, *b), specs=[VMEM] * 8)
    parts = [message] + [shift(message, z=hop) for hop in HOPS]
    a_own, b_own, vec_grad = call(
        last_kernel,
        [((16, D), BF16), ((16, D), BF16), ((8, D), F32)],
        parts,
        specs=[VMEM] * 4,
    )

    a = [a_own] + [shift(a_own, y=hop) for hop in HOPS]
    b = [b_own] + [shift(b_own, x=hop) for hop in HOPS]
    a_line, b_line = call(lines_kernel, [((64, D), BF16)] * 2, (at, *a, *b))
    a = [a_line] + [shift(a_line, x=hop) for hop in HOPS]
    b = [b_line] + [shift(b_line, y=hop) for hop in HOPS]
    pieces = a + b
    pieces = pieces + [shift(v, c=1) for v in pieces]

    other = [shift(v, c=1) for v in near]
    (state,) = call(
        state_kernel,
        [((3, D, D), BF16)],
        (at, master, moment_first, moment_second, *near, *other),
        limit=32,
    )

    vectors = jnp.stack([out_bias, ln_gain, ln_shift])
    shard = ((256, D), F32)
    rows = ((3, D), F32)
    outs = call(
        lamb_kernel,
        [((D, D), BF16), shard, shard, shard, rows, rows, rows],
        (
            at,
            *pieces,
            vec_grad,
            state,
            master,
            moment_first,
            moment_second,
            vectors,
            vector_first,
            vector_second,
        ),
        scratch=[pltpu.VMEM((D, D), BF16), pltpu.VMEM((D, D), F32)],
        limit=40,
    )
    return (d_context, d_resid, *outs)


def solution(mesh):
    tokens, copied, shard = P(("rep", "opt"), None), P(), P("opt", None)
    return jax.shard_map(
        on_device,
        mesh=mesh,
        in_specs=(tokens,) * 3 + (copied,) + (shard,) * 3 + (copied,) * 5,
        out_specs=(tokens, tokens, copied) + (shard,) * 3 + (copied,) * 3,
        check_vma=False,
    )
```

```python
import functools

import jax
import jax.numpy as jnp
from jax import lax
from jax.experimental import pallas as pl
from jax.experimental.pallas import tpu as pltpu
from jax.sharding import Mesh, PartitionSpec as P

beta_one = 0.9
beta_two = 0.999
adam_eps = 1e-06
learn_rate = 0.2
decay_rate = 0.01
max_norm = 1.0

D = 1024
BLOCK = 256
F32 = jnp.float32
BF16 = jnp.bfloat16
MIB = 1024 * 1024
AXES = ("x", "y", "c", "z")
PLANE = ("x", "y")
VMEM = pl.BlockSpec(memory_space=pltpu.VMEM)
ANY = pl.BlockSpec(memory_space=pl.ANY)
ROWS = 32
PIECE = 272


def place(x, y, c, z):
    return (((x % 4) * 4 + y % 4) * 2 + c % 2) * 4 + z % 4


def permute(value, to):
    pairs = [
        (place(x, y, c, z), place(*to(x, y, c, z)))
        for x in range(4)
        for y in range(4)
        for c in range(2)
        for z in range(4)
    ]
    return lax.ppermute(value, AXES, pairs)


def other_core(value):
    return permute(value, lambda x, y, c, z: (x, y, 1 - c, z))


def next_shard(value):
    return permute(value, lambda x, y, c, z: (x, y, c, z + 1 - 2 * c))


def exchange(value, axes):
    return lax.all_to_all(value, axes, split_axis=0, concat_axis=0, tiled=True)


def call(kernel, outs, ins, specs=None, scratch=(), cost=None, limit=58, **more):
    return pl.pallas_call(
        kernel,
        out_shape=[jax.ShapeDtypeStruct(shape, dtype) for shape, dtype in outs],
        in_specs=[VMEM] * len(ins) if specs is None else specs,
        out_specs=more.pop("out_specs", [VMEM] * len(outs)),
        scratch_shapes=list(scratch),
        cost_estimate=cost,
        compiler_params=pltpu.CompilerParams(vmem_limit_bytes=limit * MIB),
        **more,
    )(*ins)


def split_vectors(rows):
    high = rows.astype(BF16).astype(F32)
    return jnp.concatenate([high, rows - high], axis=0).astype(BF16)


def join_vectors(message):
    wide = message.astype(F32)
    return wide[0:8] + wide[8:16]


def backward_kernel(
    ctx,
    res,
    cot,
    weight,
    bias,
    gain,
    master,
    first,
    second,
    dres,
    send,
    keep,
    packed,
    ctxs,
    dress,
    pre,
    sums,
):
    step = pl.program_id(0)
    packed[0, 0] = master[...].astype(BF16)
    packed[0, 1] = first[...].astype(BF16)
    packed[0, 2] = second[...].astype(BF16)
    rows = pl.ds(pl.multiple_of(step * BLOCK, BLOCK), BLOCK)
    for shard in range(4):
        for core in range(2):
            start = 256 * shard + 128 * core
            side = 128 * (shard % 2)
            ctxs[2 * core + shard // 2, rows, side : side + 128] = ctx[:, start : start + 128]
    pre[...] = jnp.dot(ctx[...], weight[...], preferred_element_type=F32)

    @pl.when(step == 0)
    def _():
        sums[...] = jnp.zeros_like(sums)

    bias_row = bias[...]
    gain_row = gain[...]

    def chunk(i, carry):
        at_rows = pl.ds(pl.multiple_of(i * 16, 16), 16)
        value = pre[at_rows, :] + res[at_rows, :].astype(F32) + bias_row
        grad_out = cot[at_rows, :].astype(F32)
        scaled = grad_out * gain_row
        mean = jnp.sum(value, axis=1, keepdims=True) * (1.0 / D)
        mean_scaled = jnp.sum(scaled, axis=1, keepdims=True) * (1.0 / D)
        centred = value - mean
        var = jnp.sum(centred * centred, axis=1, keepdims=True) * (1.0 / D)
        cross = jnp.sum(scaled * centred, axis=1, keepdims=True) * (1.0 / D)
        rstd = lax.rsqrt(var + 1e-05)
        normed = centred * rstd
        d_pre = rstd * (scaled - mean_scaled - normed * (cross * rstd))
        d_low = d_pre.astype(BF16)
        dres[at_rows, :] = d_low
        dress[pl.ds(pl.multiple_of(step * BLOCK + i * 16, 16), 16), :] = d_low
        moved = grad_out * normed
        sums[0] += d_pre[0:8] + d_pre[8:16]
        sums[1] += moved[0:8] + moved[8:16]
        sums[2] += grad_out[0:8] + grad_out[8:16]
        return carry

    lax.fori_loop(0, BLOCK // 16, chunk, 0, unroll=2)

    @pl.when(step == D // BLOCK - 1)
    def _():
        core = lax.axis_index("c")

        def rows_of(m):
            return lax.dot_general(
                ctxs[m], dress[...], (((0,), (0,)), ((), ())), preferred_element_type=F32
            ).astype(BF16)

        for half in range(2):
            send[half * 256 : (half + 1) * 256, :] = rows_of((1 - core) * 2 + half)
        for half in range(2):
            keep[half * 256 : (half + 1) * 256, :] = rows_of(core * 2 + half)
        total = [jnp.sum(sums[k], axis=0, keepdims=True) for k in range(3)]
        message = split_vectors(jnp.concatenate(total + [jnp.zeros((5, D), F32)], axis=0))
        send[512:528, :] = message
        keep[512:528, :] = message


def backward(context, residual_in, cotangent, weight, bias, gain, master, first, second):
    block = pl.BlockSpec((BLOCK, D), lambda i: (i, 0))
    state = pl.BlockSpec((64, D), lambda i: (i, 0))
    pack = pl.BlockSpec((1, 3, 64, D), lambda i: (i // 2, 0, i % 2, 0))
    whole = pl.BlockSpec((D, D), lambda i: (0, 0))
    row = pl.BlockSpec((1, D), lambda i: (0, 0))
    half = pl.BlockSpec((528, D), lambda i: (0, 0))
    return call(
        backward_kernel,
        [((D, D), BF16), ((528, D), BF16), ((528, D), BF16), ((2, 3, 128, D), BF16)],
        (context, residual_in, cotangent, weight, bias, gain, master, first, second),
        specs=[block, block, block, whole, row, row, state, state, state],
        out_specs=[block, half, half, pack],
        grid=(D // BLOCK,),
        scratch=[
            pltpu.VMEM((4, D, 256), BF16),
            pltpu.VMEM((D, D), BF16),
            pltpu.VMEM((BLOCK, D), F32),
            pltpu.VMEM((3, 8, D), F32),
        ],
        cost=pl.CostEstimate(flops=4 * D**3, bytes_accessed=14 * MIB, transcendentals=D),
    )


def context_kernel(dres, weight, out):
    out[...] = lax.dot_general(
        dres[...], weight[...], (((1,), (1,)), ((), ())), preferred_element_type=F32
    ).astype(BF16)


def context_grad(d_resid, weight):
    block = pl.BlockSpec((BLOCK, D), lambda i: (i, 0))
    return call(
        context_kernel,
        [((D, D), BF16)],
        (d_resid, weight),
        specs=[block, pl.BlockSpec((D, D), lambda i: (0, 0))],
        out_specs=[block],
        grid=(D // BLOCK,),
        cost=pl.CostEstimate(flops=2 * D**3, bytes_accessed=6 * MIB, transcendentals=0),
    )[0]


def core_kernel(keep, got, out):
    message = split_vectors(join_vectors(keep[512:528, :]) + join_vectors(got[512:528, :]))
    for j in range(16):
        rows = slice(ROWS * j, ROWS * (j + 1))
        total = (keep[rows, :].astype(F32) + got[rows, :].astype(F32)).astype(BF16)
        for k in range(8):
            out[j, ROWS * k : ROWS * (k + 1), :] = total[:, 128 * k : 128 * (k + 1)]
        k = j % 8
        out[j, 256:PIECE, :] = message[:, 128 * k : 128 * (k + 1)]


def sum_kernel(n, copies, got, *rest):
    out = rest[-1]
    for at in range(0, 256, 32):
        rows = slice(at, at + 32)
        total = got[0, rows, :].astype(F32)
        for j in range(1, n):
            total = total + got[j, rows, :].astype(F32)
        total = total.astype(BF16)
        for j in range(copies):
            out[j, rows, :] = total
    total = join_vectors(got[0, 256:PIECE, :])
    for j in range(1, n):
        total = total + join_vectors(got[j, 256:PIECE, :])
    message = split_vectors(total)
    for j in range(copies):
        out[j, 256:PIECE, :] = message


def step_of(grad, first, second, param, decay):
    first_new = beta_one * first + (1.0 - beta_one) * grad
    second_new = beta_two * second + (1.0 - beta_two) * grad * grad
    update = first_new / (jnp.sqrt(second_new) + adam_eps) + decay * param
    return first_new, second_new, update


def lamb_kernel(
    mine,
    others,
    near,
    near_other,
    far,
    far_other,
    master,
    first,
    second,
    vectors,
    vec_first,
    vec_second,
    weight_out,
    master_out,
    first_out,
    second_out,
    vec_out,
    vec_first_out,
    vec_second_out,
    grad,
    update,
    sums,
):
    core, z = lax.axis_index("c"), lax.axis_index("z")
    for which, pieces in enumerate((mine, others)):
        half = 128 * lax.rem(core + which, 2)
        for j in range(16):
            rows = pl.ds(pl.multiple_of(256 * (j // 4) + ROWS * (j % 4) + half, ROWS), ROWS)
            for k in range(8):
                block = pieces[j, ROWS * k : ROWS * (k + 1), :]
                grad[rows, 128 * k : 128 * (k + 1)] = block
    grad_vectors = jnp.concatenate(
        [join_vectors(mine[k, 256:PIECE, :]) for k in range(8)], axis=1
    )[0:3]

    def fold(value):
        return value[0:8] + value[8:16]

    zero = jnp.zeros((8, D), F32)

    def square(i, total):
        g = grad[pl.ds(pl.multiple_of(i * 16, 16), 16), :].astype(F32)
        return total + fold(g * g)

    grad_sq = jnp.sum(lax.fori_loop(0, D // 16, square, zero, unroll=4))
    total = jnp.sqrt(
        jnp.full((1, 1), grad_sq + jnp.sum(grad_vectors * grad_vectors), F32)
    )
    factor = 1.0 / jnp.maximum(1.0, total / max_norm)

    def from_pack(pack):
        return lambda rows: tuple(pack[n, rows, :].astype(F32) for n in range(3))

    def from_shard(base):
        def load(rows):
            rows = pl.ds(base + rows.start, rows.size)
            return tuple(
                ref[rows, :].astype(BF16).astype(F32) for ref in (master, first, second)
            )

        return load

    side = 1 - 2 * core
    blocks = (
        (z, 0, from_shard(0)),
        (z, 1, from_shard(128)),
        (z - side, core, from_pack(near.at[core])),
        (z - side, 1 - core, from_pack(near.at[1 - core])),
        (z + side, 1 - core, from_pack(near_other.at[1 - core])),
        (z + side, core, from_pack(near_other.at[core])),
        (z + 2, core, from_pack(far)),
        (z + 2, 1 - core, from_pack(far_other)),
    )
    blocks = [(lax.rem(s + 4, 4) * 2 + half, load) for s, half, load in blocks]

    for index, load in blocks:

        def full(i, totals):
            rows = pl.ds(pl.multiple_of(i * 16, 16), 16)
            place_at = pl.ds(pl.multiple_of(index * 128 + i * 16, 16), 16)
            w, m, v = load(rows)
            _, _, u = step_of(grad[place_at, :].astype(F32) * factor, m, v, w, decay_rate)
            update[place_at, :] = u
            return totals[0] + fold(u * u), totals[1] + fold(w * w)

        update_sq, weight_sq = lax.fori_loop(0, 8, full, (zero, zero), unroll=2)
        sums[index, 0] = update_sq
        sums[index, 1] = weight_sq

    update_sq, weight_sq = sums[0, 0], sums[0, 1]
    for index in range(1, 8):
        update_sq = update_sq + sums[index, 0]
        weight_sq = weight_sq + sums[index, 1]
    update_sq = jnp.full((1, 1), jnp.sum(update_sq), F32)
    weight_sq = jnp.full((1, 1), jnp.sum(weight_sq), F32)
    rate = learn_rate * (jnp.sqrt(weight_sq) / jnp.sqrt(update_sq + 1e-06))

    for index, load in blocks:

        def finish(i, carry):
            rows = pl.ds(pl.multiple_of(i * 16, 16), 16)
            place_at = pl.ds(pl.multiple_of(index * 128 + i * 16, 16), 16)
            weight_out[place_at, :] = (load(rows)[0] - rate * update[place_at, :]).astype(BF16)
            return carry

        lax.fori_loop(0, 8, finish, 0, unroll=2)

    def shard(i, carry):
        rows = pl.ds(pl.multiple_of(i * 16, 16), 16)
        g = grad[pl.ds(pl.multiple_of(z * 256 + i * 16, 16), 16), :].astype(F32) * factor
        w = master[rows, :]
        first_new, second_new, u = step_of(g, first[rows, :], second[rows, :], w, decay_rate)
        first_out[rows, :] = first_new
        second_out[rows, :] = second_new
        master_out[rows, :] = w - rate * u
        return carry

    lax.fori_loop(0, 256 // 16, shard, 0, unroll=2)

    params = vectors[...]
    first_new, second_new, u = step_of(
        grad_vectors * factor, vec_first[...], vec_second[...], params, 0.0
    )
    trust = jnp.sqrt(jnp.sum(params * params, axis=1, keepdims=True)) / jnp.sqrt(
        jnp.sum(u * u, axis=1, keepdims=True) + 1e-06
    )
    vec_out[...] = params - learn_rate * trust * u
    vec_first_out[...] = first_new
    vec_second_out[...] = second_new


def on_device(
    context,
    residual_in,
    cotangent,
    weight,
    master,
    moment_first,
    moment_second,
    out_bias,
    ln_gain,
    ln_shift,
    vector_first,
    vector_second,
):
    d_resid, send, keep, packed = backward(
        context,
        residual_in,
        cotangent,
        weight,
        out_bias.reshape(1, D),
        ln_gain.reshape(1, D),
        master,
        moment_first,
        moment_second,
    )
    got = other_core(send)
    near = next_shard(packed)
    d_context = context_grad(d_resid, weight)

    (pieces,) = call(core_kernel, [((16, PIECE, 128), BF16)], (keep, got), limit=8)
    pieces = exchange(pieces, PLANE)
    (pieces,) = call(
        functools.partial(sum_kernel, 16, 4),
        [((4, PIECE, 128), BF16)],
        (pieces, near, d_context),
        specs=[VMEM, ANY, ANY],
        limit=8,
    )
    far = next_shard(lax.dynamic_index_in_dim(near, lax.axis_index("c"), keepdims=False))
    pieces = exchange(pieces, "z")
    (pieces,) = call(
        functools.partial(sum_kernel, 4, 16),
        [((16, PIECE, 128), BF16)],
        (pieces, far),
        specs=[VMEM, ANY],
        limit=8,
    )
    near_other, far_other = other_core(near), other_core(far)
    mine = exchange(pieces, PLANE)
    others = other_core(mine)

    vectors = jnp.stack([out_bias, ln_gain, ln_shift])
    shard = ((256, D), F32)
    rows = ((3, D), F32)
    outs = call(
        lamb_kernel,
        [((D, D), BF16), shard, shard, shard, rows, rows, rows],
        (
            mine,
            others,
            near,
            near_other,
            far,
            far_other,
            master,
            moment_first,
            moment_second,
            vectors,
            vector_first,
            vector_second,
        ),
        specs=[VMEM] * 12,
        scratch=[
            pltpu.VMEM((D, D), BF16),
            pltpu.VMEM((D, D), F32),
            pltpu.VMEM((8, 2, 8, D), F32),
        ],
        limit=40,
    )
    return (d_context, d_resid, *outs)


def solution(mesh):
    mesh = Mesh(mesh.devices.reshape(4, 4, 2, 4), AXES)
    tokens, copied, shard = P(AXES, None), P(), P("z", None)
    return jax.shard_map(
        on_device,
        mesh=mesh,
        in_specs=(tokens,) * 3 + (copied,) + (shard,) * 3 + (copied,) * 5,
        out_specs=(tokens, tokens, copied) + (shard,) * 3 + (copied,) * 3,
        check_vma=False,
    )
```

```python
import functools

import jax
import jax.numpy as jnp
from jax import lax
from jax.experimental import pallas as pl
from jax.experimental.pallas import tpu as pltpu
from jax.sharding import Mesh, PartitionSpec as P

beta_one = 0.9
beta_two = 0.999
adam_eps = 1e-06
learn_rate = 0.2
decay_rate = 0.01
max_norm = 1.0

D = 1024
BLOCK = 256
F32 = jnp.float32
BF16 = jnp.bfloat16
MIB = 1024 * 1024
AXES = ("x", "y", "c", "z")
PLANE = ("x", "y")
VMEM = pl.BlockSpec(memory_space=pltpu.VMEM)
ANY = pl.BlockSpec(memory_space=pl.ANY)
HBM = pl.BlockSpec(memory_space=pltpu.HBM)
DMA = pltpu.SemaphoreType.DMA
ROWS = 32
PIECE = 272


def place(x, y, c, z):
    return (((x % 4) * 4 + y % 4) * 2 + c % 2) * 4 + z % 4


def permute(value, to):
    pairs = [
        (place(x, y, c, z), place(*to(x, y, c, z)))
        for x in range(4)
        for y in range(4)
        for c in range(2)
        for z in range(4)
    ]
    return lax.ppermute(value, AXES, pairs)


def other_core(value):
    return permute(value, lambda x, y, c, z: (x, y, 1 - c, z))


def next_shard(value):
    return permute(value, lambda x, y, c, z: (x, y, c, z + 1 - 2 * c))


def exchange(value, axes):
    return lax.all_to_all(value, axes, split_axis=0, concat_axis=0, tiled=True)


def call(kernel, outs, ins, specs=None, scratch=(), cost=None, limit=58, **more):
    return pl.pallas_call(
        kernel,
        out_shape=[jax.ShapeDtypeStruct(shape, dtype) for shape, dtype in outs],
        in_specs=[VMEM] * len(ins) if specs is None else specs,
        out_specs=more.pop("out_specs", [VMEM] * len(outs)),
        scratch_shapes=list(scratch),
        cost_estimate=cost,
        compiler_params=pltpu.CompilerParams(vmem_limit_bytes=limit * MIB),
        **more,
    )(*ins)


def split_vectors(rows):
    high = rows.astype(BF16).astype(F32)
    return jnp.concatenate([high, rows - high], axis=0).astype(BF16)


def join_vectors(message):
    wide = message.astype(F32)
    return wide[0:8] + wide[8:16]


def start(source, target, semaphore):
    copy = pltpu.make_async_copy(source, target, semaphore)
    copy.start()
    return copy


def fold(value):
    return value[0:8] + value[8:16]


def layer_norm_rows(value, cotangent, gain_row):
    grad_out = cotangent.astype(F32)
    scaled = grad_out * gain_row
    mean = jnp.sum(value, axis=1, keepdims=True) * (1.0 / D)
    mean_scaled = jnp.sum(scaled, axis=1, keepdims=True) * (1.0 / D)
    centred = value - mean
    var = jnp.sum(centred * centred, axis=1, keepdims=True) * (1.0 / D)
    cross = jnp.sum(scaled * centred, axis=1, keepdims=True) * (1.0 / D)
    rstd = lax.rsqrt(var + 1e-05)
    slope = rstd * rstd * cross
    d_pre = rstd * ((scaled - mean_scaled) - centred * slope)
    return d_pre, grad_out * (centred * rstd), grad_out


def backward_kernel(
    ctx_hbm,
    res_hbm,
    cot_hbm,
    weight_hbm,
    bias,
    gain,
    master_hbm,
    first_hbm,
    second_hbm,
    dres_hbm,
    send,
    keep,
    packed,
    ctx,
    res,
    cot,
    weight,
    dres,
    pre,
    state,
    sums,
    token_sems,
    weight_sem,
    state_sems,
    out_sems,
):
    blocks = D // BLOCK
    tokens = ((ctx_hbm, ctx), (res_hbm, res), (cot_hbm, cot))

    def rows_of_block(b):
        return pl.ds(b * BLOCK, BLOCK)

    def fetch(b, n):
        source, target = tokens[n]
        rows = rows_of_block(b)
        return start(source.at[rows], target.at[rows], token_sems.at[n, b])

    def product(b):
        pre[b % 2] = jnp.dot(
            ctx[rows_of_block(b), :], weight[...], preferred_element_type=F32
        )

    first_ctx = fetch(0, 0)
    weight_copy = start(weight_hbm, weight, weight_sem)
    copies = [[first_ctx, fetch(0, 1), fetch(0, 2)]]
    bias_row = bias[...]
    gain_row = gain[...]
    sums[...] = jnp.zeros_like(sums)
    weight_copy.wait()
    copies[0][0].wait()
    copies += [[fetch(b, n) for n in range(3)] for b in range(1, blocks)]
    product(0)
    outs = []
    for b in range(blocks):
        copies[b][1].wait()
        copies[b][2].wait()
        if b == 2:
            shards = (master_hbm, first_hbm, second_hbm)
            state_copies = [start(r, state.at[n], state_sems.at[n]) for n, r in enumerate(shards)]
        if b + 1 < blocks:
            copies[b + 1][0].wait()
            product(b + 1)
        for i in range(0, BLOCK, 64):
            totals = None
            for j in range(i, i + 64, 16):
                rows = pl.ds(b * BLOCK + j, 16)
                value = pre[b % 2, j : j + 16, :] + res[rows, :].astype(F32) + bias_row
                parts = layer_norm_rows(value, cot[rows, :], gain_row)
                dres[rows, :] = parts[0].astype(BF16)
                parts = [fold(part) for part in parts]
                totals = parts if totals is None else [p + q for p, q in zip(totals, parts)]
            for k in range(3):
                sums[k] += totals[k]
        rows = rows_of_block(b)
        outs.append(start(dres.at[rows], dres_hbm.at[rows], out_sems.at[b]))

    for n, copy in enumerate(state_copies):
        copy.wait()
        for half in range(2):
            packed[half, n] = state[n, 128 * half : 128 * half + 128, :].astype(BF16)

    core = lax.axis_index("c")

    def grad_rows(which, half):
        columns = [
            pl.ds(pl.multiple_of(256 * shard + 128 * which, 128), 128)
            for shard in (2 * half, 2 * half + 1)
        ]
        left = jnp.concatenate([ctx[:, cols] for cols in columns], axis=1)
        return lax.dot_general(
            left, dres[...], (((0,), (0,)), ((), ())), preferred_element_type=F32
        ).astype(BF16)

    for half in range(2):
        send[256 * half : 256 * half + 256, :] = grad_rows(1 - core, half)
    for half in range(2):
        keep[256 * half : 256 * half + 256, :] = grad_rows(core, half)
    total = [jnp.sum(sums[k], axis=0, keepdims=True) for k in range(3)]
    message = split_vectors(jnp.concatenate(total + [jnp.zeros((5, D), F32)], axis=0))
    send[512:528, :] = message
    keep[512:528, :] = message
    for copy in outs:
        copy.wait()


def backward(context, residual_in, cotangent, weight, bias, gain, master, first, second):
    whole = pltpu.VMEM((D, D), BF16)
    return call(
        backward_kernel,
        [((D, D), BF16), ((528, D), BF16), ((528, D), BF16), ((2, 3, 128, D), BF16)],
        (context, residual_in, cotangent, weight, bias, gain, master, first, second),
        specs=[HBM] * 4 + [VMEM] * 2 + [HBM] * 3,
        out_specs=[HBM, VMEM, VMEM, VMEM],
        scratch=[whole] * 5
        + [
            pltpu.VMEM((2, BLOCK, D), F32),
            pltpu.VMEM((3, 256, D), F32),
            pltpu.VMEM((3, 8, D), F32),
            DMA((3, D // BLOCK)),
            DMA,
            DMA((3,)),
            DMA((D // BLOCK,)),
        ],
        cost=pl.CostEstimate(flops=4 * D**3, bytes_accessed=0, transcendentals=0),
        limit=58,
    )


def context_kernel(dres, weight, out, token):
    token[...] = jnp.zeros_like(token)
    out[...] = lax.dot_general(
        dres[...], weight[...], (((1,), (1,)), ((), ())), preferred_element_type=F32
    ).astype(BF16)


def context_grad(d_resid, weight):
    block = pl.BlockSpec((BLOCK, D), lambda i: (i, 0))
    return call(
        context_kernel,
        [((D, D), BF16), ((8, 128), F32)],
        (d_resid, weight),
        specs=[block, pl.BlockSpec((D, D), lambda i: (0, 0))],
        out_specs=[block, pl.BlockSpec((8, 128), lambda i: (0, 0))],
        grid=(D // BLOCK,),
        cost=pl.CostEstimate(flops=2 * D**3, bytes_accessed=0, transcendentals=0),
        limit=24,
    )


def pass_kernel(packed, out):
    pass


def core_kernel(keep, got, out):
    message = split_vectors(join_vectors(keep[512:528, :]) + join_vectors(got[512:528, :]))
    for j in range(16):
        rows = slice(ROWS * j, ROWS * (j + 1))
        total = (keep[rows, :].astype(F32) + got[rows, :].astype(F32)).astype(BF16)
        for k in range(8):
            out[j, ROWS * k : ROWS * (k + 1), :] = total[:, 128 * k : 128 * (k + 1)]
        k = j % 8
        out[j, 256:PIECE, :] = message[:, 128 * k : 128 * (k + 1)]


def sum_kernel(n, copies, got, *rest):
    out = rest[-1]
    for at in range(0, 256, 32):
        rows = slice(at, at + 32)
        total = got[0, rows, :].astype(F32)
        for j in range(1, n):
            total = total + got[j, rows, :].astype(F32)
        total = total.astype(BF16)
        for j in range(copies):
            out[j, rows, :] = total
    total = join_vectors(got[0, 256:PIECE, :])
    for j in range(1, n):
        total = total + join_vectors(got[j, 256:PIECE, :])
    message = split_vectors(total)
    for j in range(copies):
        out[j, 256:PIECE, :] = message


def step_of(grad, first, second, param, decay):
    first_new = beta_one * first + (1.0 - beta_one) * grad
    second_new = beta_two * second + (1.0 - beta_two) * (grad * grad)
    scale = second_new * lax.rsqrt(second_new) + adam_eps
    inverse = pl.reciprocal(scale, approx=True)
    inverse = inverse * (2.0 - scale * inverse)
    update = first_new * inverse
    return first_new, second_new, update if decay == 0.0 else update + decay * param


def stage_kernel(
    near, near_other, far, far_other, master, first, second, state, shards, weight_sq
):
    core, z = lax.axis_index("c"), lax.axis_index("z")
    side = 1 - 2 * core
    shards[0] = master[...]
    shards[1] = first[...]
    shards[2] = second[...]
    own = pl.ds(pl.multiple_of(256 * z, 256), 256)
    for n, shard in enumerate((master, first, second)):
        state[n, own, :] = shard[...].astype(BF16)
    blocks = (
        (z - side, core, near.at[core]),
        (z - side, 1 - core, near.at[1 - core]),
        (z + side, 1 - core, near_other.at[1 - core]),
        (z + side, core, near_other.at[core]),
        (z + 2, core, far),
        (z + 2, 1 - core, far_other),
    )
    for shard, half, block in blocks:
        at = 256 * lax.rem(shard + 4, 4) + 128 * half
        state[:, pl.ds(pl.multiple_of(at, 128), 128), :] = block[...]

    def square(i, total):
        wide = state[0, pl.ds(pl.multiple_of(i * 32, 32), 32), :].astype(F32)
        wide = wide * wide
        return total + (fold(wide[0:16]) + fold(wide[16:32]))

    weight_sq[...] = lax.fori_loop(0, D // 32, square, jnp.zeros((8, D), F32), unroll=2)


def half_kernel(pieces, weight_sq, token, half):
    squares = jnp.zeros((16, 128), F32)
    for j in range(16):
        for k in range(8):
            block = pieces[j, ROWS * k : ROWS * (k + 1), :]
            half[ROWS * j : ROWS * (j + 1), 128 * k : 128 * (k + 1)] = block
            wide = block.astype(F32)
            wide = wide * wide
            squares = squares + (wide[0:16] + wide[16:32])
    vectors = jnp.concatenate(
        [join_vectors(pieces[k, 256:PIECE, :]) for k in range(8)], axis=1
    )
    row = jnp.full((1, D), jnp.sum(squares), F32)
    half[512:528, :] = split_vectors(
        jnp.concatenate([vectors[0:3], row, jnp.zeros((4, D), F32)], axis=0)
    )


def lamb_kernel(
    mine,
    others,
    state_hbm,
    shard_hbm,
    weight_sq,
    vectors,
    vec_first,
    vec_second,
    weight_hbm,
    master_hbm,
    first_hbm,
    second_hbm,
    vec_out,
    vec_first_out,
    vec_second_out,
    update,
    own_update,
    sums,
    shard_out,
    weight,
    state,
    shard,
    state_sems,
    shard_sem,
    out_sems,
):
    shard_copy = start(shard_hbm, shard, shard_sem)
    state_copies = []
    for n in range(4):
        rows = pl.ds(256 * n, 256)
        state_copies.append(start(state_hbm.at[:, rows], state.at[:, rows], state_sems.at[n]))
    core, z = lax.axis_index("c"), lax.axis_index("z")
    halves = (mine, others)
    tails = [join_vectors(half[512:528, :]) for half in halves]
    grad_vectors = tails[0][0:3]
    total = jnp.sqrt(
        tails[0][3:4, 0:1]
        + tails[1][3:4, 0:1]
        + jnp.full((1, 1), jnp.sum(grad_vectors * grad_vectors), F32)
    )
    factor = 1.0 / jnp.maximum(1.0, total / max_norm)
    sums[...] = jnp.zeros_like(sums)
    shard_copy.wait()

    for which, half in enumerate(halves):
        side = lax.rem(core + which, 2)

        def own(i, carry):
            rows = pl.ds(pl.multiple_of(i * 16 + 128 * side, 16), 16)
            at = pl.ds(pl.multiple_of(128 * z + i * 16, 16), 16)
            first_new, second_new, u = step_of(
                half[at, :].astype(F32) * factor,
                shard[1, rows, :],
                shard[2, rows, :],
                shard[0, rows, :],
                decay_rate,
            )
            shard_out[1, rows, :] = first_new
            shard_out[2, rows, :] = second_new
            own_update[rows, :] = u
            return carry

        lax.fori_loop(0, 8, own, 0, unroll=2)
    outs = [
        start(shard_out.at[n], ref, out_sems.at[n])
        for n, ref in ((1, first_hbm), (2, second_hbm))
    ]

    for shard_at in range(4):
        state_copies[shard_at].wait()
        for which, half in enumerate(halves):
            side = lax.rem(core + which, 2)

            def full(i, total):
                part = pl.multiple_of(i * 16, 16)
                at = pl.ds(pl.multiple_of(256 * shard_at + 128 * side + part, 16), 16)
                g = half[pl.ds(128 * shard_at + part, 16), :].astype(F32) * factor
                w, m, v = [state[n, at, :].astype(F32) for n in range(3)]
                u = step_of(g, m, v, w, decay_rate)[2]
                update[at, :] = u
                return total + fold(u * u)

            sums[side] = lax.fori_loop(0, 8, full, sums[side], unroll=2)

    update_sq = jnp.full((1, 1), jnp.sum(sums[0] + sums[1]), F32)
    norm = jnp.sqrt(jnp.full((1, 1), jnp.sum(weight_sq[...]), F32))
    rate = learn_rate * (norm / jnp.sqrt(update_sq + 1e-06))

    def finish_shard(i, carry):
        rows = pl.ds(pl.multiple_of(i * 32, 32), 32)
        shard_out[0, rows, :] = shard[0, rows, :] - rate * own_update[rows, :]
        return carry

    lax.fori_loop(0, 8, finish_shard, 0, unroll=2)
    outs.append(start(shard_out.at[0], master_hbm, out_sems.at[0]))
    for part in range(4):

        def finish(i, carry):
            rows = pl.ds(pl.multiple_of(part * 256 + i * 32, 32), 32)
            weight[rows, :] = (state[0, rows, :].astype(F32) - rate * update[rows, :]).astype(BF16)
            return carry

        lax.fori_loop(0, 8, finish, 0, unroll=2)
        rows = pl.ds(part * 256, 256)
        outs.append(start(weight.at[rows], weight_hbm.at[rows], out_sems.at[3 + part]))

    params = vectors[...]
    first_new, second_new, u = step_of(
        grad_vectors * factor, vec_first[...], vec_second[...], params, 0.0
    )
    trust = jnp.sqrt(jnp.sum(params * params, axis=1, keepdims=True)) / jnp.sqrt(
        jnp.sum(u * u, axis=1, keepdims=True) + 1e-06
    )
    vec_out[...] = params - learn_rate * trust * u
    vec_first_out[...] = first_new
    vec_second_out[...] = second_new
    for copy in outs:
        copy.wait()


def on_device(
    context,
    residual_in,
    cotangent,
    weight,
    master,
    moment_first,
    moment_second,
    out_bias,
    ln_gain,
    ln_shift,
    vector_first,
    vector_second,
):
    d_resid, send, keep, packed = backward(
        context,
        residual_in,
        cotangent,
        weight,
        out_bias.reshape(1, D),
        ln_gain.reshape(1, D),
        master,
        moment_first,
        moment_second,
    )
    got = other_core(send)
    (packed,) = call(
        pass_kernel,
        [((2, 3, 128, D), BF16)],
        (packed,),
        specs=[ANY],
        out_specs=[ANY],
        input_output_aliases={0: 0},
        cost=pl.CostEstimate(flops=4 * D**3, bytes_accessed=0, transcendentals=0),
        limit=58,
    )
    near = next_shard(packed)
    d_context, token = context_grad(d_resid, weight)

    (pieces,) = call(core_kernel, [((16, PIECE, 128), BF16)], (keep, got), limit=8)
    pieces = exchange(pieces, PLANE)
    (pieces,) = call(
        functools.partial(sum_kernel, 16, 4),
        [((4, PIECE, 128), BF16)],
        (pieces,),
        limit=8,
    )
    far = next_shard(lax.dynamic_index_in_dim(near, lax.axis_index("c"), keepdims=False))
    pieces = exchange(pieces, "z")
    (pieces,) = call(
        functools.partial(sum_kernel, 4, 16),
        [((16, PIECE, 128), BF16)],
        (pieces,),
        limit=8,
    )
    near_other, far_other = other_core(near), other_core(far)
    pieces = exchange(pieces, PLANE)
    shard = ((256, D), F32)
    rows = ((3, D), F32)
    state, shards, weight_sq = call(
        stage_kernel,
        [((3, D, D), BF16), ((3, 256, D), F32), ((8, D), F32)],
        (near, near_other, far, far_other, master, moment_first, moment_second),
        cost=pl.CostEstimate(flops=D**3, bytes_accessed=16 * MIB, transcendentals=0),
        limit=58,
    )
    (mine,) = call(
        half_kernel,
        [((528, D), BF16)],
        (pieces, weight_sq, token),
        specs=[VMEM, ANY, ANY],
        limit=8,
    )
    others = other_core(mine)

    vectors = jnp.stack([out_bias, ln_gain, ln_shift])
    outs = call(
        lamb_kernel,
        [((D, D), BF16), shard, shard, shard, rows, rows, rows],
        (mine, others, state, shards, weight_sq, vectors, vector_first, vector_second),
        specs=[VMEM] * 2 + [HBM] * 2 + [VMEM] * 4,
        out_specs=[HBM] * 4 + [VMEM] * 3,
        scratch=[
            pltpu.VMEM((D, D), F32),
            pltpu.VMEM((256, D), F32),
            pltpu.VMEM((2, 8, D), F32),
            pltpu.VMEM((3, 256, D), F32),
            pltpu.VMEM((D, D), BF16),
            pltpu.VMEM((3, D, D), BF16),
            pltpu.VMEM((3, 256, D), F32),
            DMA((4,)),
            DMA,
            DMA((7,)),
        ],
        limit=50,
    )
    return (d_context, d_resid, *outs)


def solution(mesh):
    mesh = Mesh(mesh.devices.reshape(4, 4, 2, 4), AXES)
    tokens, copied, shard = P(AXES, None), P(), P("z", None)
    return jax.shard_map(
        on_device,
        mesh=mesh,
        in_specs=(tokens,) * 3 + (copied,) + (shard,) * 3 + (copied,) * 5,
        out_specs=(tokens, tokens, copied) + (shard,) * 3 + (copied,) * 3,
        check_vma=False,
    )
```

```python
import functools

import jax
import jax.numpy as jnp
from jax import lax
from jax.experimental import pallas as pl
from jax.experimental.pallas import tpu as pltpu
from jax.sharding import Mesh, PartitionSpec as P

beta_one = 0.9
beta_two = 0.999
adam_eps = 1e-06
learn_rate = 0.2
decay_rate = 0.01
max_norm = 1.0

D = 1024
BLOCK = 256
carried = (1.0, beta_one, beta_two)
F32 = jnp.float32
BF16 = jnp.bfloat16
MIB = 1024 * 1024
AXES = ("x", "y", "c", "z")
PLANE = ("x", "y")
VMEM = pl.BlockSpec(memory_space=pltpu.VMEM)
ANY = pl.BlockSpec(memory_space=pl.ANY)
HBM = pl.BlockSpec(memory_space=pltpu.HBM)
DMA = pltpu.SemaphoreType.DMA
ROWS = 32
PIECE = 272


def place(x, y, c, z):
    return (((x % 4) * 4 + y % 4) * 2 + c % 2) * 4 + z % 4


def permute(value, to):
    pairs = [
        (place(x, y, c, z), place(*to(x, y, c, z)))
        for x in range(4)
        for y in range(4)
        for c in range(2)
        for z in range(4)
    ]
    return lax.ppermute(value, AXES, pairs)


def other_core(value):
    return permute(value, lambda x, y, c, z: (x, y, 1 - c, z))


def next_shard(value):
    return permute(value, lambda x, y, c, z: (x, y, c, z + 1 - 2 * c))


def exchange(value, axes):
    return lax.all_to_all(value, axes, split_axis=0, concat_axis=0, tiled=True)


def call(kernel, outs, ins, specs=None, scratch=(), cost=None, limit=58, **more):
    return pl.pallas_call(
        kernel,
        out_shape=[jax.ShapeDtypeStruct(shape, dtype) for shape, dtype in outs],
        in_specs=[VMEM] * len(ins) if specs is None else specs,
        out_specs=more.pop("out_specs", [VMEM] * len(outs)),
        scratch_shapes=list(scratch),
        cost_estimate=cost,
        compiler_params=pltpu.CompilerParams(vmem_limit_bytes=limit * MIB),
        **more,
    )(*ins)


def split_vectors(rows):
    high = rows.astype(BF16).astype(F32)
    return jnp.concatenate([high, rows - high], axis=0).astype(BF16)


def join_vectors(message):
    wide = message.astype(F32)
    return wide[0:8] + wide[8:16]


def start(source, target, semaphore):
    copy = pltpu.make_async_copy(source, target, semaphore)
    copy.start()
    return copy


def fold(value):
    return value[0:8] + value[8:16]


def layer_norm_rows(value, cotangent, gain_row):
    grad_out = cotangent.astype(F32)
    scaled = grad_out * gain_row
    mean = jnp.sum(value, axis=1, keepdims=True) * (1.0 / D)
    mean_scaled = jnp.sum(scaled, axis=1, keepdims=True) * (1.0 / D)
    centred = value - mean
    var = jnp.sum(centred * centred, axis=1, keepdims=True) * (1.0 / D)
    cross = jnp.sum(scaled * centred, axis=1, keepdims=True) * (1.0 / D)
    rstd = lax.rsqrt(var + 1e-05)
    slope = rstd * rstd * cross
    d_pre = rstd * ((scaled - mean_scaled) - centred * slope)
    return d_pre, grad_out * (centred * rstd), grad_out


def backward_kernel(
    ctx_hbm,
    res_hbm,
    cot_hbm,
    weight_hbm,
    bias,
    gain,
    master_hbm,
    first_hbm,
    second_hbm,
    dres_hbm,
    send_hbm,
    keep_hbm,
    packed_hbm,
    send,
    keep,
    packed,
    ctx,
    res,
    cot,
    weight,
    dres,
    pre,
    state,
    sums,
    token_sems,
    weight_sem,
    state_sems,
    out_sems,
):
    blocks = D // BLOCK
    tokens = ((ctx_hbm, ctx), (res_hbm, res), (cot_hbm, cot))

    def rows_of_block(b):
        return pl.ds(b * BLOCK, BLOCK)

    def fetch(b, n):
        source, target = tokens[n]
        rows = rows_of_block(b)
        return start(source.at[rows], target.at[rows], token_sems.at[n, b])

    def product(b):
        pre[b % 2] = jnp.dot(
            ctx[rows_of_block(b), :], weight[...], preferred_element_type=F32
        )

    first_ctx = fetch(0, 0)
    weight_copy = start(weight_hbm, weight, weight_sem)
    copies = [[first_ctx, fetch(0, 1), fetch(0, 2)]]
    bias_row = bias[...]
    gain_row = gain[...]
    sums[...] = jnp.zeros_like(sums)
    weight_copy.wait()
    copies[0][0].wait()
    copies += [[fetch(b, n) for n in range(3)] for b in range(1, blocks)]
    product(0)
    outs = []
    for b in range(blocks):
        copies[b][1].wait()
        copies[b][2].wait()
        if b == 2:
            shards = (master_hbm, first_hbm, second_hbm)
            state_copies = [start(r, state.at[n], state_sems.at[n]) for n, r in enumerate(shards)]
        if b + 1 < blocks:
            copies[b + 1][0].wait()
            product(b + 1)
        for i in range(0, BLOCK, 64):
            totals = None
            for j in range(i, i + 64, 16):
                rows = pl.ds(b * BLOCK + j, 16)
                value = pre[b % 2, j : j + 16, :] + res[rows, :].astype(F32) + bias_row
                parts = layer_norm_rows(value, cot[rows, :], gain_row)
                dres[rows, :] = parts[0].astype(BF16)
                parts = [fold(part) for part in parts]
                totals = parts if totals is None else [p + q for p, q in zip(totals, parts)]
            for k in range(3):
                sums[k] += totals[k]
        rows = rows_of_block(b)
        outs.append(start(dres.at[rows], dres_hbm.at[rows], out_sems.at[b]))

    for n, copy in enumerate(state_copies):
        copy.wait()
        for half in range(2):
            rows = slice(128 * half, 128 * half + 128)
            packed[half, n] = (state[n, rows, :] * carried[n]).astype(BF16)
    outs.append(start(packed, packed_hbm, out_sems.at[blocks]))

    core = lax.axis_index("c")

    def grad_rows(which, half):
        columns = [
            pl.ds(pl.multiple_of(256 * shard + 128 * which, 128), 128)
            for shard in (2 * half, 2 * half + 1)
        ]
        left = jnp.concatenate([ctx[:, cols] for cols in columns], axis=1)
        return lax.dot_general(
            left, dres[...], (((0,), (0,)), ((), ())), preferred_element_type=F32
        ).astype(BF16)

    total = [jnp.sum(sums[k], axis=0, keepdims=True) for k in range(3)]
    message = split_vectors(jnp.concatenate(total + [jnp.zeros((5, D), F32)], axis=0))
    halves = ((send, send_hbm, 1 - core), (keep, keep_hbm, core))
    for n, (half, target, which) in enumerate(halves):
        half[512:528, :] = message
        for part in range(2):
            half[256 * part : 256 * part + 256, :] = grad_rows(which, part)
            rows = pl.ds(256 * part, 256 + 16 * part)
            outs.append(start(half.at[rows], target.at[rows], out_sems.at[blocks + 1 + 2 * n + part]))
    for copy in outs:
        copy.wait()


def backward(context, residual_in, cotangent, weight, bias, gain, master, first, second):
    whole = pltpu.VMEM((D, D), BF16)
    return call(
        backward_kernel,
        [((D, D), BF16), ((528, D), BF16), ((528, D), BF16), ((2, 3, 128, D), BF16)],
        (context, residual_in, cotangent, weight, bias, gain, master, first, second),
        specs=[HBM] * 4 + [VMEM] * 2 + [HBM] * 3,
        out_specs=[HBM] * 4,
        scratch=[pltpu.VMEM((528, D), BF16)] * 2
        + [pltpu.VMEM((2, 3, 128, D), BF16)]
        + [whole] * 5
        + [
            pltpu.VMEM((2, BLOCK, D), F32),
            pltpu.VMEM((3, 256, D), F32),
            pltpu.VMEM((3, 8, D), F32),
            DMA((3, D // BLOCK)),
            DMA,
            DMA((3,)),
            DMA((D // BLOCK + 5,)),
        ],
        cost=pl.CostEstimate(flops=4 * D**3, bytes_accessed=0, transcendentals=0),
        limit=58,
    )


def context_kernel(dres, weight, out, token):
    token[...] = jnp.zeros_like(token)
    out[...] = lax.dot_general(
        dres[...], weight[...], (((1,), (1,)), ((), ())), preferred_element_type=F32
    ).astype(BF16)


def context_grad(d_resid, weight):
    block = pl.BlockSpec((BLOCK, D), lambda i: (i, 0))
    return call(
        context_kernel,
        [((D, D), BF16), ((8, 128), F32)],
        (d_resid, weight),
        specs=[block, pl.BlockSpec((D, D), lambda i: (0, 0))],
        out_specs=[block, pl.BlockSpec((8, 128), lambda i: (0, 0))],
        grid=(D // BLOCK,),
        cost=pl.CostEstimate(flops=2 * D**3, bytes_accessed=0, transcendentals=0),
        limit=24,
    )


def pass_kernel(value, out):
    pass


def token_kernel(value, token):
    token[...] = jnp.zeros_like(token)


def core_kernel(keep, got, out):
    message = split_vectors(join_vectors(keep[512:528, :]) + join_vectors(got[512:528, :]))
    for j in range(16):
        rows = slice(ROWS * j, ROWS * (j + 1))
        total = (keep[rows, :].astype(F32) + got[rows, :].astype(F32)).astype(BF16)
        for k in range(8):
            out[j, ROWS * k : ROWS * (k + 1), :] = total[:, 128 * k : 128 * (k + 1)]
        k = j % 8
        out[j, 256:PIECE, :] = message[:, 128 * k : 128 * (k + 1)]


def sum_kernel(n, copies, got, *rest):
    out = rest[-1]
    for at in range(0, 256, 32):
        rows = slice(at, at + 32)
        total = got[0, rows, :].astype(F32)
        for j in range(1, n):
            total = total + got[j, rows, :].astype(F32)
        total = total.astype(BF16)
        for j in range(copies):
            out[j, rows, :] = total
    total = join_vectors(got[0, 256:PIECE, :])
    for j in range(1, n):
        total = total + join_vectors(got[j, 256:PIECE, :])
    message = split_vectors(total)
    for j in range(copies):
        out[j, 256:PIECE, :] = message


def step_of(grad, first, second, param, decay):
    first_new = beta_one * first + (1.0 - beta_one) * grad
    second_new = beta_two * second + (1.0 - beta_two) * (grad * grad)
    scale = second_new * lax.rsqrt(second_new) + adam_eps
    inverse = pl.reciprocal(scale, approx=True)
    inverse = inverse * (2.0 - scale * inverse)
    update = first_new * inverse
    return first_new, second_new, update if decay == 0.0 else update + decay * param


def stage_kernel(
    near, near_other, far, far_other, master, first, second, w_out, m_out, v_out, weight_sq
):
    core, z = lax.axis_index("c"), lax.axis_index("z")
    side = 1 - 2 * core
    own = pl.ds(pl.multiple_of(256 * z, 256), 256)
    state = (w_out, m_out, v_out)
    for out, shard, scale in zip(state, (master, first, second), carried):
        out[own, :] = (shard[...] * scale).astype(BF16)
    blocks = (
        (z - side, core, near.at[core]),
        (z - side, 1 - core, near.at[1 - core]),
        (z + side, 1 - core, near_other.at[1 - core]),
        (z + side, core, near_other.at[core]),
        (z + 2, core, far),
        (z + 2, 1 - core, far_other),
    )
    for shard, half, block in blocks:
        at = 256 * lax.rem(shard + 4, 4) + 128 * half
        rows = pl.ds(pl.multiple_of(at, 128), 128)
        for n, out in enumerate(state):
            out[rows, :] = block[n]

    def square(i, total):
        wide = w_out[pl.ds(pl.multiple_of(i * 32, 32), 32), :].astype(F32)
        wide = wide * wide
        return total + (fold(wide[0:16]) + fold(wide[16:32]))

    weight_sq[...] = lax.fori_loop(0, D // 32, square, jnp.zeros((8, D), F32), unroll=2)


def half_kernel(pieces, weight_sq, half):
    squares = jnp.zeros((16, 128), F32)
    for j in range(16):
        for k in range(8):
            block = pieces[j, ROWS * k : ROWS * (k + 1), :]
            half[ROWS * j : ROWS * (j + 1), 128 * k : 128 * (k + 1)] = block
            wide = block.astype(F32)
            wide = wide * wide
            squares = squares + (wide[0:16] + wide[16:32])
    vectors = jnp.concatenate(
        [join_vectors(pieces[k, 256:PIECE, :]) for k in range(8)], axis=1
    )
    row = jnp.full((1, D), jnp.sum(squares), F32)
    half[512:528, :] = split_vectors(
        jnp.concatenate([vectors[0:3], row, jnp.zeros((4, D), F32)], axis=0)
    )


def lamb_kernel(
    mine,
    others,
    w_in,
    m_in,
    v_in,
    master,
    first,
    second,
    weight_sq,
    vectors,
    vec_first,
    vec_second,
    token,
    weight_hbm,
    master_hbm,
    first_hbm,
    second_hbm,
    vec_out,
    vec_first_out,
    vec_second_out,
    update,
    own_update,
    sums,
    shard_out,
    weight,
    out_sems,
):
    core, z = lax.axis_index("c"), lax.axis_index("z")
    halves = (mine, others)
    tails = [join_vectors(half[512:528, :]) for half in halves]
    grad_vectors = tails[0][0:3]
    total = jnp.sqrt(
        tails[0][3:4, 0:1]
        + tails[1][3:4, 0:1]
        + jnp.full((1, 1), jnp.sum(grad_vectors * grad_vectors), F32)
    )
    factor = 1.0 / jnp.maximum(1.0, total / max_norm)
    first_rate = (1.0 - beta_one) * factor
    second_rate = (1.0 - beta_two) * (factor * factor)
    sums[...] = jnp.zeros_like(sums)
    for which, half in enumerate(halves):
        side = lax.rem(core + which, 2)

        def own(i, carry):
            rows = pl.ds(pl.multiple_of(i * 16 + 128 * side, 16), 16)
            at = pl.ds(pl.multiple_of(128 * z + i * 16, 16), 16)
            first_new, second_new, u = step_of(
                half[at, :].astype(F32) * factor,
                first[rows, :],
                second[rows, :],
                master[rows, :],
                decay_rate,
            )
            shard_out[1, rows, :] = first_new
            shard_out[2, rows, :] = second_new
            own_update[rows, :] = u
            return carry

        lax.fori_loop(0, 8, own, 0, unroll=2)
    outs = [
        start(shard_out.at[n], ref, out_sems.at[n])
        for n, ref in ((1, first_hbm), (2, second_hbm))
    ]

    for shard_at in range(4):
        for which, half in enumerate(halves):
            side = lax.rem(core + which, 2)

            def full(i, total):
                part = pl.multiple_of(i * 16, 16)
                at = pl.ds(pl.multiple_of(256 * shard_at + 128 * side + part, 16), 16)
                g = half[pl.ds(128 * shard_at + part, 16), :].astype(F32)
                w, m, v = [ref[at, :].astype(F32) for ref in (w_in, m_in, v_in)]
                second_new = v + second_rate * (g * g)
                scale = second_new * lax.rsqrt(second_new) + adam_eps
                u = (m + first_rate * g) * pl.reciprocal(scale, approx=True) + decay_rate * w
                update[at, :] = u
                return total + fold(u * u)

            sums[side] = lax.fori_loop(0, 8, full, sums[side], unroll=4)

    update_sq = jnp.full((1, 1), jnp.sum(sums[0] + sums[1]), F32)
    norm = jnp.sqrt(jnp.full((1, 1), jnp.sum(weight_sq[...]), F32))
    rate = learn_rate * (norm / jnp.sqrt(update_sq + 1e-06))

    def finish_shard(i, carry):
        rows = pl.ds(pl.multiple_of(i * 32, 32), 32)
        shard_out[0, rows, :] = master[rows, :] - rate * own_update[rows, :]
        return carry

    lax.fori_loop(0, 8, finish_shard, 0, unroll=2)
    outs.append(start(shard_out.at[0], master_hbm, out_sems.at[0]))
    for part in range(4):

        def finish(i, carry):
            rows = pl.ds(pl.multiple_of(part * 256 + i * 32, 32), 32)
            weight[rows, :] = (w_in[rows, :].astype(F32) - rate * update[rows, :]).astype(BF16)
            return carry

        lax.fori_loop(0, 8, finish, 0, unroll=2)
        rows = pl.ds(part * 256, 256)
        outs.append(start(weight.at[rows], weight_hbm.at[rows], out_sems.at[3 + part]))

    params = vectors[...]
    first_new, second_new, u = step_of(
        grad_vectors * factor, vec_first[...], vec_second[...], params, 0.0
    )
    trust = jnp.sqrt(jnp.sum(params * params, axis=1, keepdims=True)) / jnp.sqrt(
        jnp.sum(u * u, axis=1, keepdims=True) + 1e-06
    )
    vec_out[...] = params - learn_rate * trust * u
    vec_first_out[...] = first_new
    vec_second_out[...] = second_new
    for copy in outs:
        copy.wait()


def on_device(
    context,
    residual_in,
    cotangent,
    weight,
    master,
    moment_first,
    moment_second,
    out_bias,
    ln_gain,
    ln_shift,
    vector_first,
    vector_second,
):
    d_resid, send, keep, packed = backward(
        context,
        residual_in,
        cotangent,
        weight,
        out_bias.reshape(1, D),
        ln_gain.reshape(1, D),
        master,
        moment_first,
        moment_second,
    )
    got = other_core(send)
    (packed,) = call(
        pass_kernel,
        [((2, 3, 128, D), BF16)],
        (packed,),
        specs=[ANY],
        out_specs=[ANY],
        input_output_aliases={0: 0},
        cost=pl.CostEstimate(flops=4 * D**3, bytes_accessed=0, transcendentals=0),
        limit=58,
    )
    near = next_shard(packed)
    d_context, token = context_grad(d_resid, weight)

    (pieces,) = call(core_kernel, [((16, PIECE, 128), BF16)], (keep, got), limit=8)
    pieces = exchange(pieces, PLANE)
    (pieces,) = call(
        functools.partial(sum_kernel, 16, 4),
        [((4, PIECE, 128), BF16)],
        (pieces,),
        limit=8,
    )
    half_at = lax.axis_index("c") + token[0, 0].astype(jnp.int32)
    far = next_shard(lax.dynamic_index_in_dim(near, half_at, keepdims=False))
    pieces = exchange(pieces, "z")
    (pieces,) = call(
        functools.partial(sum_kernel, 4, 16),
        [((16, PIECE, 128), BF16)],
        (pieces,),
        limit=8,
    )
    near_other, far_other = other_core(near), other_core(far)
    pieces = exchange(pieces, PLANE)
    shard = ((256, D), F32)
    rows = ((3, D), F32)
    *state, weight_sq = call(
        stage_kernel,
        [((D, D), BF16)] * 3 + [((8, D), F32)],
        (near, near_other, far, far_other, master, moment_first, moment_second),
        cost=pl.CostEstimate(flops=D**3, bytes_accessed=16 * MIB, transcendentals=0),
        limit=53,
    )
    (mine,) = call(
        half_kernel,
        [((528, D), BF16)],
        (pieces, weight_sq),
        specs=[VMEM, ANY],
        limit=8,
    )
    others = other_core(mine)
    (token,) = call(
        token_kernel,
        [((8, 128), F32)],
        (mine,),
        specs=[ANY],
        cost=pl.CostEstimate(flops=30 * D**3, bytes_accessed=0, transcendentals=0),
        limit=16,
    )

    vectors = jnp.stack([out_bias, ln_gain, ln_shift])
    outs = call(
        lamb_kernel,
        [((D, D), BF16), shard, shard, shard, rows, rows, rows],
        (
            mine,
            others,
            *state,
            master,
            moment_first,
            moment_second,
            weight_sq,
            vectors,
            vector_first,
            vector_second,
            token,
        ),
        out_specs=[HBM] * 4 + [VMEM] * 3,
        scratch=[
            pltpu.VMEM((D, D), F32),
            pltpu.VMEM((256, D), F32),
            pltpu.VMEM((2, 8, D), F32),
            pltpu.VMEM((3, 256, D), F32),
            pltpu.VMEM((D, D), BF16),
            DMA((7,)),
        ],
        limit=28,
    )
    return (d_context, d_resid, *outs)


def solution(mesh):
    mesh = Mesh(mesh.devices.reshape(4, 4, 2, 4), AXES)
    tokens, copied, shard = P(AXES, None), P(), P("z", None)
    return jax.shard_map(
        on_device,
        mesh=mesh,
        in_specs=(tokens,) * 3 + (copied,) + (shard,) * 3 + (copied,) * 5,
        out_specs=(tokens, tokens, copied) + (shard,) * 3 + (copied,) * 3,
        check_vma=False,
    )
```

```python
import functools

import jax
import jax.numpy as jnp
from jax import lax
from jax.experimental import pallas as pl
from jax.experimental.pallas import tpu as pltpu
from jax.sharding import Mesh, PartitionSpec as P

beta_one = 0.9
beta_two = 0.999
adam_eps = 1e-06
learn_rate = 0.2
decay_rate = 0.01
max_norm = 1.0

D = 1024
BLOCK = 256
carried = (1.0, beta_one, beta_two)
F32 = jnp.float32
BF16 = jnp.bfloat16
MIB = 1024 * 1024
AXES = ("x", "y", "c", "z")
VMEM = pl.BlockSpec(memory_space=pltpu.VMEM)
ANY = pl.BlockSpec(memory_space=pl.ANY)
HBM = pl.BlockSpec(memory_space=pltpu.HBM)
DMA = pltpu.SemaphoreType.DMA
ROWS = 32
PIECE = 272


def place(x, y, c, z):
    return (((x % 4) * 4 + y % 4) * 2 + c % 2) * 4 + z % 4


def permute(value, to):
    pairs = [
        (place(x, y, c, z), place(*to(x, y, c, z)))
        for x in range(4)
        for y in range(4)
        for c in range(2)
        for z in range(4)
    ]
    return lax.ppermute(value, AXES, pairs)


def other_core(value):
    return permute(value, lambda x, y, c, z: (x, y, 1 - c, z))


def next_shard(value):
    return permute(value, lambda x, y, c, z: (x, y, c, z + 1 - 2 * c))


def order(n, core):
    return range(n - 1, -1, -1) if core else range(n)


def exchange(value, groups):
    return lax.all_to_all(
        value, AXES, split_axis=0, concat_axis=0, axis_index_groups=groups, tiled=True
    )


def exchange_plane(value):
    return exchange(
        value,
        [[place(n // 4, n % 4, c, z) for n in order(16, c)] for c in range(2) for z in range(4)],
    )


def exchange_z(value):
    return exchange(
        value,
        [
            [place(x, y, c, z) for z in order(4, c)]
            for x in range(4)
            for y in range(4)
            for c in range(2)
        ],
    )


def call(kernel, outs, ins, specs=None, scratch=(), cost=None, limit=58, **more):
    return pl.pallas_call(
        kernel,
        out_shape=[jax.ShapeDtypeStruct(shape, dtype) for shape, dtype in outs],
        in_specs=[VMEM] * len(ins) if specs is None else specs,
        out_specs=more.pop("out_specs", [VMEM] * len(outs)),
        scratch_shapes=list(scratch),
        cost_estimate=cost,
        compiler_params=pltpu.CompilerParams(vmem_limit_bytes=limit * MIB),
        **more,
    )(*ins)


def split_vectors(rows):
    high = rows.astype(BF16).astype(F32)
    return jnp.concatenate([high, rows - high], axis=0).astype(BF16)


def join_vectors(message):
    wide = message.astype(F32)
    return wide[0:8] + wide[8:16]


def start(source, target, semaphore):
    copy = pltpu.make_async_copy(source, target, semaphore)
    copy.start()
    return copy


def fold(value):
    return value[0:8] + value[8:16]


def layer_norm_rows(value, cotangent, gain_row):
    grad_out = cotangent.astype(F32)
    scaled = grad_out * gain_row
    mean = jnp.sum(value, axis=1, keepdims=True) * (1.0 / D)
    mean_scaled = jnp.sum(scaled, axis=1, keepdims=True) * (1.0 / D)
    centred = value - mean
    var = jnp.sum(centred * centred, axis=1, keepdims=True) * (1.0 / D)
    cross = jnp.sum(scaled * centred, axis=1, keepdims=True) * (1.0 / D)
    rstd = lax.rsqrt(var + 1e-05)
    slope = rstd * rstd * cross
    d_pre = rstd * ((scaled - mean_scaled) - centred * slope)
    return d_pre, grad_out * (centred * rstd), grad_out


def backward_kernel(
    ctx_hbm,
    res_hbm,
    cot_hbm,
    weight_hbm,
    bias,
    gain,
    master_hbm,
    first_hbm,
    second_hbm,
    dres_hbm,
    send_hbm,
    keep_hbm,
    packed_hbm,
    send,
    keep,
    packed,
    ctx,
    res,
    cot,
    weight,
    dres,
    pre,
    state,
    sums,
    token_sems,
    weight_sem,
    state_sems,
    out_sems,
):
    blocks = D // BLOCK
    tokens = ((ctx_hbm, ctx), (res_hbm, res), (cot_hbm, cot))

    def rows_of_block(b):
        return pl.ds(b * BLOCK, BLOCK)

    def fetch(b, n):
        source, target = tokens[n]
        rows = rows_of_block(b)
        return start(source.at[rows], target.at[rows], token_sems.at[n, b])

    def product(b):
        pre[b % 2] = jnp.dot(
            ctx[rows_of_block(b), :], weight[...], preferred_element_type=F32
        )

    first_ctx = fetch(0, 0)
    weight_copy = start(weight_hbm, weight, weight_sem)
    copies = [[first_ctx, fetch(0, 1), fetch(0, 2)]]
    bias_row = bias[...]
    gain_row = gain[...]
    sums[...] = jnp.zeros_like(sums)
    weight_copy.wait()
    copies[0][0].wait()
    copies += [[fetch(b, n) for n in range(3)] for b in range(1, blocks)]
    product(0)
    outs = []
    for b in range(blocks):
        copies[b][1].wait()
        copies[b][2].wait()
        if b == 2:
            shards = (master_hbm, first_hbm, second_hbm)
            state_copies = [start(r, state.at[n], state_sems.at[n]) for n, r in enumerate(shards)]
        if b + 1 < blocks:
            copies[b + 1][0].wait()
            product(b + 1)
        for i in range(0, BLOCK, 64):
            totals = None
            for j in range(i, i + 64, 16):
                rows = pl.ds(b * BLOCK + j, 16)
                value = pre[b % 2, j : j + 16, :] + res[rows, :].astype(F32) + bias_row
                parts = layer_norm_rows(value, cot[rows, :], gain_row)
                dres[rows, :] = parts[0].astype(BF16)
                parts = [fold(part) for part in parts]
                totals = parts if totals is None else [p + q for p, q in zip(totals, parts)]
            for k in range(3):
                sums[k] += totals[k]
        rows = rows_of_block(b)
        outs.append(start(dres.at[rows], dres_hbm.at[rows], out_sems.at[b]))

    for n, copy in enumerate(state_copies):
        copy.wait()
        for half in range(2):
            rows = slice(128 * half, 128 * half + 128)
            packed[half, n] = (state[n, rows, :] * carried[n]).astype(BF16)
    outs.append(start(packed, packed_hbm, out_sems.at[blocks]))

    core = lax.axis_index("c")

    def grad_rows(which, half):
        columns = [
            pl.ds(pl.multiple_of(256 * shard + 128 * which, 128), 128)
            for shard in (2 * half, 2 * half + 1)
        ]
        left = jnp.concatenate([ctx[:, cols] for cols in columns], axis=1)
        return lax.dot_general(
            left, dres[...], (((0,), (0,)), ((), ())), preferred_element_type=F32
        ).astype(BF16)

    total = [jnp.sum(sums[k], axis=0, keepdims=True) for k in range(3)]
    message = split_vectors(jnp.concatenate(total + [jnp.zeros((5, D), F32)], axis=0))
    halves = ((send, send_hbm, 1 - core), (keep, keep_hbm, core))
    for n, (half, target, which) in enumerate(halves):
        half[512:528, :] = message
        for part in range(2):
            half[256 * part : 256 * part + 256, :] = grad_rows(which, part)
            rows = pl.ds(256 * part, 256 + 16 * part)
            outs.append(start(half.at[rows], target.at[rows], out_sems.at[blocks + 1 + 2 * n + part]))
    for copy in outs:
        copy.wait()


def backward(context, residual_in, cotangent, weight, bias, gain, master, first, second):
    whole = pltpu.VMEM((D, D), BF16)
    return call(
        backward_kernel,
        [((D, D), BF16), ((528, D), BF16), ((528, D), BF16), ((2, 3, 128, D), BF16)],
        (context, residual_in, cotangent, weight, bias, gain, master, first, second),
        specs=[HBM] * 4 + [VMEM] * 2 + [HBM] * 3,
        out_specs=[HBM] * 4,
        scratch=[pltpu.VMEM((528, D), BF16)] * 2
        + [pltpu.VMEM((2, 3, 128, D), BF16)]
        + [whole] * 5
        + [
            pltpu.VMEM((2, BLOCK, D), F32),
            pltpu.VMEM((3, 256, D), F32),
            pltpu.VMEM((3, 8, D), F32),
            DMA((3, D // BLOCK)),
            DMA,
            DMA((3,)),
            DMA((D // BLOCK + 5,)),
        ],
        cost=pl.CostEstimate(flops=4 * D**3, bytes_accessed=0, transcendentals=0),
        limit=58,
    )


def context_kernel(dres, weight, out, token):
    token[...] = jnp.zeros_like(token)
    out[...] = lax.dot_general(
        dres[...], weight[...], (((1,), (1,)), ((), ())), preferred_element_type=F32
    ).astype(BF16)


def context_grad(d_resid, weight):
    block = pl.BlockSpec((BLOCK, D), lambda i: (i, 0))
    return call(
        context_kernel,
        [((D, D), BF16), ((8, 128), F32)],
        (d_resid, weight),
        specs=[block, pl.BlockSpec((D, D), lambda i: (0, 0))],
        out_specs=[block, pl.BlockSpec((8, 128), lambda i: (0, 0))],
        grid=(D // BLOCK,),
        cost=pl.CostEstimate(flops=2 * D**3, bytes_accessed=0, transcendentals=0),
        limit=24,
    )


def pass_kernel(value, out):
    pass


def token_kernel(value, token):
    token[...] = jnp.zeros_like(token)


def core_kernel(keep, got, out):
    message = split_vectors(join_vectors(keep[512:528, :]) + join_vectors(got[512:528, :]))
    for j in range(16):
        rows = slice(ROWS * j, ROWS * (j + 1))
        total = (keep[rows, :].astype(F32) + got[rows, :].astype(F32)).astype(BF16)
        for k in range(8):
            out[j, ROWS * k : ROWS * (k + 1), :] = total[:, 128 * k : 128 * (k + 1)]
        k = j % 8
        out[j, 256:PIECE, :] = message[:, 128 * k : 128 * (k + 1)]


def sum_kernel(n, copies, got, *rest):
    out = rest[-1]
    for at in range(0, 256, 32):
        rows = slice(at, at + 32)
        total = got[0, rows, :].astype(F32)
        for j in range(1, n):
            total = total + got[j, rows, :].astype(F32)
        total = total.astype(BF16)
        for j in range(copies):
            out[j, rows, :] = total
    total = join_vectors(got[0, 256:PIECE, :])
    for j in range(1, n):
        total = total + join_vectors(got[j, 256:PIECE, :])
    message = split_vectors(total)
    for j in range(copies):
        out[j, 256:PIECE, :] = message


def step_of(grad, first, second, param, decay):
    first_new = beta_one * first + (1.0 - beta_one) * grad
    second_new = beta_two * second + (1.0 - beta_two) * (grad * grad)
    scale = second_new * lax.rsqrt(second_new) + adam_eps
    inverse = pl.reciprocal(scale, approx=True)
    inverse = inverse * (2.0 - scale * inverse)
    update = first_new * inverse
    return first_new, second_new, update if decay == 0.0 else update + decay * param


def stage_kernel(
    near, near_other, far, far_other, master, first, second, w_out, m_out, v_out, weight_sq
):
    core, z = lax.axis_index("c"), lax.axis_index("z")
    side = 1 - 2 * core
    own = pl.ds(pl.multiple_of(256 * z, 256), 256)
    state = (w_out, m_out, v_out)
    for out, shard, scale in zip(state, (master, first, second), carried):
        out[own, :] = (shard[...] * scale).astype(BF16)
    blocks = (
        (z - side, core, near.at[core]),
        (z - side, 1 - core, near.at[1 - core]),
        (z + side, 1 - core, near_other.at[1 - core]),
        (z + side, core, near_other.at[core]),
        (z + 2, core, far),
        (z + 2, 1 - core, far_other),
    )
    for shard, half, block in blocks:
        at = 256 * lax.rem(shard + 4, 4) + 128 * half
        rows = pl.ds(pl.multiple_of(at, 128), 128)
        for n, out in enumerate(state):
            out[rows, :] = block[n]

    def square(i, total):
        wide = w_out[pl.ds(pl.multiple_of(i * 32, 32), 32), :].astype(F32)
        wide = wide * wide
        return total + (fold(wide[0:16]) + fold(wide[16:32]))

    weight_sq[...] = lax.fori_loop(0, D // 32, square, jnp.zeros((8, D), F32), unroll=2)


def half_kernel(pieces, weight_sq, half):
    squares = jnp.zeros((16, 128), F32)
    for j in range(16):
        for k in range(8):
            block = pieces[j, ROWS * k : ROWS * (k + 1), :]
            half[ROWS * j : ROWS * (j + 1), 128 * k : 128 * (k + 1)] = block
            wide = block.astype(F32)
            wide = wide * wide
            squares = squares + (wide[0:16] + wide[16:32])
    vectors = jnp.concatenate(
        [join_vectors(pieces[k, 256:PIECE, :]) for k in range(8)], axis=1
    )
    row = jnp.full((1, D), jnp.sum(squares), F32)
    half[512:528, :] = split_vectors(
        jnp.concatenate([vectors[0:3], row, jnp.zeros((4, D), F32)], axis=0)
    )


def lamb_kernel(
    mine,
    others,
    w_in,
    m_in,
    v_in,
    master,
    first,
    second,
    weight_sq,
    vectors,
    vec_first,
    vec_second,
    token,
    weight_hbm,
    master_hbm,
    first_hbm,
    second_hbm,
    vec_out,
    vec_first_out,
    vec_second_out,
    update,
    own_update,
    sums,
    shard_out,
    weight,
    out_sems,
):
    core, z = lax.axis_index("c"), lax.axis_index("z")
    halves = (mine, others)
    tails = [join_vectors(half[512:528, :]) for half in halves]
    grad_vectors = jnp.where(core == 0, tails[0], tails[1])[0:3]
    total = jnp.sqrt(
        tails[0][3:4, 0:1]
        + tails[1][3:4, 0:1]
        + jnp.full((1, 1), jnp.sum(grad_vectors * grad_vectors), F32)
    )
    factor = 1.0 / jnp.maximum(1.0, total / max_norm)
    first_rate = (1.0 - beta_one) * factor
    second_rate = (1.0 - beta_two) * (factor * factor)
    sums[...] = jnp.zeros_like(sums)
    for which, half in enumerate(halves):
        side = lax.rem(core + which, 2)

        def own(i, carry):
            rows = pl.ds(pl.multiple_of(i * 16 + 128 * side, 16), 16)
            at = pl.ds(pl.multiple_of(128 * z + i * 16, 16), 16)
            first_new, second_new, u = step_of(
                half[at, :].astype(F32) * factor,
                first[rows, :],
                second[rows, :],
                master[rows, :],
                decay_rate,
            )
            shard_out[1, rows, :] = first_new
            shard_out[2, rows, :] = second_new
            own_update[rows, :] = u
            return carry

        lax.fori_loop(0, 8, own, 0, unroll=2)
    outs = [
        start(shard_out.at[n], ref, out_sems.at[n])
        for n, ref in ((1, first_hbm), (2, second_hbm))
    ]

    for shard_at in range(4):
        for which, half in enumerate(halves):
            side = lax.rem(core + which, 2)

            def full(i, total):
                part = pl.multiple_of(i * 16, 16)
                at = pl.ds(pl.multiple_of(256 * shard_at + 128 * side + part, 16), 16)
                g = half[pl.ds(128 * shard_at + part, 16), :].astype(F32)
                w, m, v = [ref[at, :].astype(F32) for ref in (w_in, m_in, v_in)]
                second_new = v + second_rate * (g * g)
                scale = second_new * lax.rsqrt(second_new) + adam_eps
                u = (m + first_rate * g) * pl.reciprocal(scale, approx=True) + decay_rate * w
                update[at, :] = u
                return total + fold(u * u)

            sums[side] = lax.fori_loop(0, 8, full, sums[side], unroll=4)

    update_sq = jnp.full((1, 1), jnp.sum(sums[0] + sums[1]), F32)
    norm = jnp.sqrt(jnp.full((1, 1), jnp.sum(weight_sq[...]), F32))
    rate = learn_rate * (norm / jnp.sqrt(update_sq + 1e-06))

    def finish_shard(i, carry):
        rows = pl.ds(pl.multiple_of(i * 32, 32), 32)
        shard_out[0, rows, :] = master[rows, :] - rate * own_update[rows, :]
        return carry

    lax.fori_loop(0, 8, finish_shard, 0, unroll=2)
    outs.append(start(shard_out.at[0], master_hbm, out_sems.at[0]))
    for part in range(4):

        def finish(i, carry):
            rows = pl.ds(pl.multiple_of(part * 256 + i * 32, 32), 32)
            weight[rows, :] = (w_in[rows, :].astype(F32) - rate * update[rows, :]).astype(BF16)
            return carry

        lax.fori_loop(0, 8, finish, 0, unroll=2)
        rows = pl.ds(part * 256, 256)
        outs.append(start(weight.at[rows], weight_hbm.at[rows], out_sems.at[3 + part]))

    params = vectors[...]
    first_new, second_new, u = step_of(
        grad_vectors * factor, vec_first[...], vec_second[...], params, 0.0
    )
    trust = jnp.sqrt(jnp.sum(params * params, axis=1, keepdims=True)) / jnp.sqrt(
        jnp.sum(u * u, axis=1, keepdims=True) + 1e-06
    )
    vec_out[...] = params - learn_rate * trust * u
    vec_first_out[...] = first_new
    vec_second_out[...] = second_new
    for copy in outs:
        copy.wait()


def on_device(
    context,
    residual_in,
    cotangent,
    weight,
    master,
    moment_first,
    moment_second,
    out_bias,
    ln_gain,
    ln_shift,
    vector_first,
    vector_second,
):
    d_resid, send, keep, packed = backward(
        context,
        residual_in,
        cotangent,
        weight,
        out_bias.reshape(1, D),
        ln_gain.reshape(1, D),
        master,
        moment_first,
        moment_second,
    )
    got = other_core(send)
    (packed,) = call(
        pass_kernel,
        [((2, 3, 128, D), BF16)],
        (packed,),
        specs=[ANY],
        out_specs=[ANY],
        input_output_aliases={0: 0},
        cost=pl.CostEstimate(flops=4 * D**3, bytes_accessed=0, transcendentals=0),
        limit=58,
    )
    near = next_shard(packed)
    d_context, token = context_grad(d_resid, weight)

    (pieces,) = call(core_kernel, [((16, PIECE, 128), BF16)], (keep, got), limit=8)
    pieces = exchange_plane(pieces)
    (pieces,) = call(
        functools.partial(sum_kernel, 16, 4),
        [((4, PIECE, 128), BF16)],
        (pieces,),
        limit=8,
    )
    half_at = lax.axis_index("c") + token[0, 0].astype(jnp.int32)
    far = next_shard(lax.dynamic_index_in_dim(near, half_at, keepdims=False))
    pieces = exchange_z(pieces)
    (pieces,) = call(
        functools.partial(sum_kernel, 4, 16),
        [((16, PIECE, 128), BF16)],
        (pieces,),
        limit=8,
    )
    near_other, far_other = other_core(near), other_core(far)
    pieces = exchange_plane(pieces)
    shard = ((256, D), F32)
    rows = ((3, D), F32)
    *state, weight_sq = call(
        stage_kernel,
        [((D, D), BF16)] * 3 + [((8, D), F32)],
        (near, near_other, far, far_other, master, moment_first, moment_second),
        cost=pl.CostEstimate(flops=D**3, bytes_accessed=16 * MIB, transcendentals=0),
        limit=53,
    )
    (mine,) = call(
        half_kernel,
        [((528, D), BF16)],
        (pieces, weight_sq),
        specs=[VMEM, ANY],
        limit=8,
    )
    others = other_core(mine)
    (token,) = call(
        token_kernel,
        [((8, 128), F32)],
        (mine,),
        specs=[ANY],
        cost=pl.CostEstimate(flops=30 * D**3, bytes_accessed=0, transcendentals=0),
        limit=16,
    )

    vectors = jnp.stack([out_bias, ln_gain, ln_shift])
    outs = call(
        lamb_kernel,
        [((D, D), BF16), shard, shard, shard, rows, rows, rows],
        (
            mine,
            others,
            *state,
            master,
            moment_first,
            moment_second,
            weight_sq,
            vectors,
            vector_first,
            vector_second,
            token,
        ),
        out_specs=[HBM] * 4 + [VMEM] * 3,
        scratch=[
            pltpu.VMEM((D, D), F32),
            pltpu.VMEM((256, D), F32),
            pltpu.VMEM((2, 8, D), F32),
            pltpu.VMEM((3, 256, D), F32),
            pltpu.VMEM((D, D), BF16),
            DMA((7,)),
        ],
        limit=28,
    )
    return (d_context, d_resid, *outs)


def solution(mesh):
    mesh = Mesh(mesh.devices.reshape(4, 4, 2, 4), AXES)
    tokens, copied, shard = P(AXES, None), P(), P("z", None)
    return jax.shard_map(
        on_device,
        mesh=mesh,
        in_specs=(tokens,) * 3 + (copied,) + (shard,) * 3 + (copied,) * 5,
        out_specs=(tokens, tokens, copied) + (shard,) * 3 + (copied,) * 3,
        check_vma=False,
    )
```

```python
import functools

import jax
import jax.numpy as jnp
from jax import lax
from jax.experimental import pallas as pl
from jax.experimental.pallas import tpu as pltpu
from jax.sharding import Mesh, PartitionSpec as P

beta_one = 0.9
beta_two = 0.999
adam_eps = 1e-06
learn_rate = 0.2
decay_rate = 0.01
max_norm = 1.0

D = 1024
BLOCK = 256
carried = (1.0, beta_one, beta_two)
F32 = jnp.float32
BF16 = jnp.bfloat16
MIB = 1024 * 1024
AXES = ("x", "y", "c", "z")
VMEM = pl.BlockSpec(memory_space=pltpu.VMEM)
ANY = pl.BlockSpec(memory_space=pl.ANY)
HBM = pl.BlockSpec(memory_space=pltpu.HBM)
DMA = pltpu.SemaphoreType.DMA
ROWS = 32
PIECE = 272


def place(x, y, c, z):
    return (((x % 4) * 4 + y % 4) * 2 + c % 2) * 4 + z % 4


def permute(value, to):
    pairs = [
        (place(x, y, c, z), place(*to(x, y, c, z)))
        for x in range(4)
        for y in range(4)
        for c in range(2)
        for z in range(4)
    ]
    return lax.ppermute(value, AXES, pairs)


def other_core(value):
    return permute(value, lambda x, y, c, z: (x, y, 1 - c, z))


def next_shard(value):
    return permute(value, lambda x, y, c, z: (x, y, c, z + 1 - 2 * c))


def order(n, core):
    return range(n - 1, -1, -1) if core else range(n)


def exchange(value, groups):
    return lax.all_to_all(
        value, AXES, split_axis=0, concat_axis=0, axis_index_groups=groups, tiled=True
    )


def exchange_plane(value):
    return exchange(
        value,
        [[place(n // 4, n % 4, c, z) for n in order(16, c)] for c in range(2) for z in range(4)],
    )


def exchange_z(value):
    return exchange(
        value,
        [
            [place(x, y, c, z) for z in order(4, c)]
            for x in range(4)
            for y in range(4)
            for c in range(2)
        ],
    )


def call(kernel, outs, ins, specs=None, scratch=(), cost=None, limit=58, **more):
    return pl.pallas_call(
        kernel,
        out_shape=[jax.ShapeDtypeStruct(shape, dtype) for shape, dtype in outs],
        in_specs=[VMEM] * len(ins) if specs is None else specs,
        out_specs=more.pop("out_specs", [VMEM] * len(outs)),
        scratch_shapes=list(scratch),
        cost_estimate=cost,
        compiler_params=pltpu.CompilerParams(vmem_limit_bytes=limit * MIB),
        **more,
    )(*ins)


def split_vectors(rows):
    high = rows.astype(BF16).astype(F32)
    return jnp.concatenate([high, rows - high], axis=0).astype(BF16)


def join_vectors(message):
    wide = message.astype(F32)
    return wide[0:8] + wide[8:16]


def start(source, target, semaphore):
    copy = pltpu.make_async_copy(source, target, semaphore)
    copy.start()
    return copy


def fold(value):
    return value[0:8] + value[8:16]


def layer_norm_rows(value, cotangent, gain_row):
    grad_out = cotangent.astype(F32)
    scaled = grad_out * gain_row
    mean = jnp.sum(value, axis=1, keepdims=True) * (1.0 / D)
    mean_scaled = jnp.sum(scaled, axis=1, keepdims=True) * (1.0 / D)
    centred = value - mean
    var = jnp.sum(centred * centred, axis=1, keepdims=True) * (1.0 / D)
    cross = jnp.sum(scaled * centred, axis=1, keepdims=True) * (1.0 / D)
    rstd = lax.rsqrt(var + 1e-05)
    slope = rstd * rstd * cross
    d_pre = rstd * ((scaled - mean_scaled) - centred * slope)
    return d_pre, grad_out * (centred * rstd), grad_out


def backward_kernel(
    ctx_hbm,
    res_hbm,
    cot_hbm,
    weight_hbm,
    bias,
    gain,
    master_hbm,
    first_hbm,
    second_hbm,
    dres_hbm,
    send_hbm,
    keep_hbm,
    packed_hbm,
    send,
    keep,
    packed,
    ctx,
    res,
    cot,
    weight,
    dres,
    pre,
    state,
    sums,
    token_sems,
    weight_sems,
    state_sems,
    out_sems,
):
    blocks = D // BLOCK
    tokens = ((ctx_hbm, ctx), (res_hbm, res), (cot_hbm, cot))

    def rows_of_block(b):
        return pl.ds(b * BLOCK, BLOCK)

    def fetch(b, n):
        source, target = tokens[n]
        rows = rows_of_block(b)
        return start(source.at[rows], target.at[rows], token_sems.at[n, b])

    def product(b):
        pre[b % 2] = jnp.dot(
            ctx[rows_of_block(b), :], weight[...], preferred_element_type=F32
        )

    first_ctx = fetch(0, 0)
    weight_copies = []
    for b in range(blocks):
        rows = rows_of_block(b)
        weight_copies.append(start(weight_hbm.at[rows], weight.at[rows], weight_sems.at[b]))
    copies = [[first_ctx, fetch(0, 1), fetch(0, 2)]]
    bias_row = bias[...]
    gain_row = gain[...]
    sums[...] = jnp.zeros_like(sums)
    for copy in weight_copies:
        copy.wait()
    copies[0][0].wait()
    copies += [[fetch(b, n) for n in range(3)] for b in range(1, blocks)]
    product(0)
    outs = []
    for b in range(blocks):
        copies[b][1].wait()
        copies[b][2].wait()
        if b == 1:
            shards = (master_hbm, first_hbm, second_hbm)
            state_copies = [start(r, state.at[n], state_sems.at[n]) for n, r in enumerate(shards)]
        if b + 1 < blocks:
            copies[b + 1][0].wait()
            product(b + 1)
        if b + 1 == blocks:
            for n, copy in enumerate(state_copies):
                copy.wait()
                for half in range(2):
                    rows = slice(128 * half, 128 * half + 128)
                    packed[half, n] = (state[n, rows, :] * carried[n]).astype(BF16)
            outs.append(start(packed, packed_hbm, out_sems.at[blocks]))
        for i in range(0, BLOCK, 64):
            totals = None
            for j in range(i, i + 64, 16):
                rows = pl.ds(b * BLOCK + j, 16)
                value = pre[b % 2, j : j + 16, :] + res[rows, :].astype(F32) + bias_row
                parts = layer_norm_rows(value, cot[rows, :], gain_row)
                dres[rows, :] = parts[0].astype(BF16)
                parts = [fold(part) for part in parts]
                totals = parts if totals is None else [p + q for p, q in zip(totals, parts)]
            for k in range(3):
                sums[k] += totals[k]
        rows = rows_of_block(b)
        outs.append(start(dres.at[rows], dres_hbm.at[rows], out_sems.at[b]))

    core = lax.axis_index("c")

    def grad_rows(which, half):
        columns = [
            pl.ds(pl.multiple_of(256 * shard + 128 * which, 128), 128)
            for shard in (2 * half, 2 * half + 1)
        ]
        left = jnp.concatenate([ctx[:, cols] for cols in columns], axis=1)
        return lax.dot_general(
            left, dres[...], (((0,), (0,)), ((), ())), preferred_element_type=F32
        ).astype(BF16)

    total = [jnp.sum(sums[k], axis=0, keepdims=True) for k in range(3)]
    message = split_vectors(jnp.concatenate(total + [jnp.zeros((5, D), F32)], axis=0))
    halves = ((send, send_hbm, 1 - core), (keep, keep_hbm, core))
    for n, (half, target, which) in enumerate(halves):
        half[512:528, :] = message
        for part in range(2):
            half[256 * part : 256 * part + 256, :] = grad_rows(which, part)
            rows = pl.ds(256 * part, 256 + 16 * part)
            outs.append(start(half.at[rows], target.at[rows], out_sems.at[blocks + 1 + 2 * n + part]))
    for copy in outs:
        copy.wait()


def backward(context, residual_in, cotangent, weight, bias, gain, master, first, second):
    whole = pltpu.VMEM((D, D), BF16)
    return call(
        backward_kernel,
        [((D, D), BF16), ((528, D), BF16), ((528, D), BF16), ((2, 3, 128, D), BF16)],
        (context, residual_in, cotangent, weight, bias, gain, master, first, second),
        specs=[HBM] * 4 + [VMEM] * 2 + [HBM] * 3,
        out_specs=[HBM] * 4,
        scratch=[pltpu.VMEM((528, D), BF16)] * 2
        + [pltpu.VMEM((2, 3, 128, D), BF16)]
        + [whole] * 5
        + [
            pltpu.VMEM((2, BLOCK, D), F32),
            pltpu.VMEM((3, 256, D), F32),
            pltpu.VMEM((3, 8, D), F32),
            DMA((3, D // BLOCK)),
            DMA((D // BLOCK,)),
            DMA((3,)),
            DMA((D // BLOCK + 5,)),
        ],
        cost=pl.CostEstimate(flops=4 * D**3, bytes_accessed=0, transcendentals=0),
        limit=58,
    )


def context_kernel(dres, weight, out, token):
    token[...] = jnp.zeros_like(token)
    out[...] = lax.dot_general(
        dres[...], weight[...], (((1,), (1,)), ((), ())), preferred_element_type=F32
    ).astype(BF16)


def context_grad(d_resid, weight):
    block = pl.BlockSpec((BLOCK, D), lambda i: (i, 0))
    return call(
        context_kernel,
        [((D, D), BF16), ((8, 128), F32)],
        (d_resid, weight),
        specs=[block, pl.BlockSpec((D, D), lambda i: (0, 0))],
        out_specs=[block, pl.BlockSpec((8, 128), lambda i: (0, 0))],
        grid=(D // BLOCK,),
        cost=pl.CostEstimate(flops=2 * D**3, bytes_accessed=0, transcendentals=0),
        limit=24,
    )


def pass_kernel(value, out):
    pass


def token_kernel(value, token):
    token[...] = jnp.zeros_like(token)


def core_kernel(keep, got, out):
    message = split_vectors(join_vectors(keep[512:528, :]) + join_vectors(got[512:528, :]))
    for j in range(16):
        rows = slice(ROWS * j, ROWS * (j + 1))
        total = (keep[rows, :].astype(F32) + got[rows, :].astype(F32)).astype(BF16)
        for k in range(8):
            out[j, ROWS * k : ROWS * (k + 1), :] = total[:, 128 * k : 128 * (k + 1)]
        k = j % 8
        out[j, 256:PIECE, :] = message[:, 128 * k : 128 * (k + 1)]


def sum_kernel(n, copies, got, *rest):
    out = rest[-1]
    for at in range(0, 256, 32):
        rows = slice(at, at + 32)
        total = got[0, rows, :].astype(F32)
        for j in range(1, n):
            total = total + got[j, rows, :].astype(F32)
        total = total.astype(BF16)
        for j in range(copies):
            out[j, rows, :] = total
    total = join_vectors(got[0, 256:PIECE, :])
    for j in range(1, n):
        total = total + join_vectors(got[j, 256:PIECE, :])
    message = split_vectors(total)
    for j in range(copies):
        out[j, 256:PIECE, :] = message


def step_of(grad, first, second, param, decay):
    first_new = beta_one * first + (1.0 - beta_one) * grad
    second_new = beta_two * second + (1.0 - beta_two) * (grad * grad)
    scale = second_new * lax.rsqrt(second_new) + adam_eps
    inverse = pl.reciprocal(scale, approx=True)
    inverse = inverse * (2.0 - scale * inverse)
    update = first_new * inverse
    return first_new, second_new, update if decay == 0.0 else update + decay * param


def stage_kernel(
    near, near_other, far, far_other, master, first, second, w_out, m_out, v_out, weight_sq
):
    core, z = lax.axis_index("c"), lax.axis_index("z")
    side = 1 - 2 * core
    own = pl.ds(pl.multiple_of(256 * z, 256), 256)
    state = (w_out, m_out, v_out)
    for out, shard, scale in zip(state, (master, first, second), carried):
        out[own, :] = (shard[...] * scale).astype(BF16)
    blocks = (
        (z - side, core, near.at[core]),
        (z - side, 1 - core, near.at[1 - core]),
        (z + side, 1 - core, near_other.at[1 - core]),
        (z + side, core, near_other.at[core]),
        (z + 2, core, far),
        (z + 2, 1 - core, far_other),
    )
    for shard, half, block in blocks:
        at = 256 * lax.rem(shard + 4, 4) + 128 * half
        rows = pl.ds(pl.multiple_of(at, 128), 128)
        for n, out in enumerate(state):
            out[rows, :] = block[n]

    def square(i, total):
        wide = w_out[pl.ds(pl.multiple_of(i * 32, 32), 32), :].astype(F32)
        wide = wide * wide
        return total + (fold(wide[0:16]) + fold(wide[16:32]))

    weight_sq[...] = lax.fori_loop(0, D // 32, square, jnp.zeros((8, D), F32), unroll=2)


def half_kernel(pieces, weight_sq, half):
    squares = jnp.zeros((16, 128), F32)
    for j in range(16):
        for k in range(8):
            block = pieces[j, ROWS * k : ROWS * (k + 1), :]
            half[ROWS * j : ROWS * (j + 1), 128 * k : 128 * (k + 1)] = block
            wide = block.astype(F32)
            wide = wide * wide
            squares = squares + (wide[0:16] + wide[16:32])
    vectors = jnp.concatenate(
        [join_vectors(pieces[k, 256:PIECE, :]) for k in range(8)], axis=1
    )
    row = jnp.full((1, D), jnp.sum(squares), F32)
    half[512:528, :] = split_vectors(
        jnp.concatenate([vectors[0:3], row, jnp.zeros((4, D), F32)], axis=0)
    )


def lamb_kernel(
    mine,
    others,
    w_in,
    m_in,
    v_in,
    master,
    first,
    second,
    weight_sq,
    vectors,
    vec_first,
    vec_second,
    token,
    weight_hbm,
    master_hbm,
    first_hbm,
    second_hbm,
    vec_out,
    vec_first_out,
    vec_second_out,
    update,
    own_update,
    sums,
    shard_out,
    weight,
    out_sems,
):
    core, z = lax.axis_index("c"), lax.axis_index("z")
    halves = (mine, others)
    tails = [join_vectors(half[512:528, :]) for half in halves]
    grad_vectors = jnp.where(core == 0, tails[0], tails[1])[0:3]
    total = jnp.sqrt(
        tails[0][3:4, 0:1]
        + tails[1][3:4, 0:1]
        + jnp.full((1, 1), jnp.sum(grad_vectors * grad_vectors), F32)
    )
    factor = 1.0 / jnp.maximum(1.0, total / max_norm)
    first_rate = (1.0 - beta_one) * factor
    second_rate = (1.0 - beta_two) * (factor * factor)
    sums[...] = jnp.zeros_like(sums)
    for which, half in enumerate(halves):
        side = lax.rem(core + which, 2)

        def own(i, carry):
            rows = pl.ds(pl.multiple_of(i * 16 + 128 * side, 16), 16)
            at = pl.ds(pl.multiple_of(128 * z + i * 16, 16), 16)
            first_new, second_new, u = step_of(
                half[at, :].astype(F32) * factor,
                first[rows, :],
                second[rows, :],
                master[rows, :],
                decay_rate,
            )
            shard_out[1, rows, :] = first_new
            shard_out[2, rows, :] = second_new
            own_update[rows, :] = u
            return carry

        lax.fori_loop(0, 8, own, 0, unroll=2)
    outs = [
        start(shard_out.at[n], ref, out_sems.at[n])
        for n, ref in ((1, first_hbm), (2, second_hbm))
    ]

    for shard_at in range(4):
        for which, half in enumerate(halves):
            side = lax.rem(core + which, 2)

            def full(i, total):
                part = pl.multiple_of(i * 16, 16)
                at = pl.ds(pl.multiple_of(256 * shard_at + 128 * side + part, 16), 16)
                g = half[pl.ds(128 * shard_at + part, 16), :].astype(F32)
                w, m, v = [ref[at, :].astype(F32) for ref in (w_in, m_in, v_in)]
                second_new = v + second_rate * (g * g)
                scale = second_new * lax.rsqrt(second_new) + adam_eps
                u = (m + first_rate * g) * pl.reciprocal(scale, approx=True) + decay_rate * w
                update[at, :] = u
                return total + fold(u * u)

            sums[side] = lax.fori_loop(0, 8, full, sums[side], unroll=8)

    update_sq = jnp.full((1, 1), jnp.sum(sums[0] + sums[1]), F32)
    norm = jnp.sqrt(jnp.full((1, 1), jnp.sum(weight_sq[...]), F32))
    rate = learn_rate * (norm / jnp.sqrt(update_sq + 1e-06))

    def finish_shard(i, carry):
        rows = pl.ds(pl.multiple_of(i * 32, 32), 32)
        shard_out[0, rows, :] = master[rows, :] - rate * own_update[rows, :]
        return carry

    lax.fori_loop(0, 8, finish_shard, 0, unroll=2)
    outs.append(start(shard_out.at[0], master_hbm, out_sems.at[0]))
    for part in range(4):

        def finish(i, carry):
            rows = pl.ds(pl.multiple_of(part * 256 + i * 32, 32), 32)
            weight[rows, :] = (w_in[rows, :].astype(F32) - rate * update[rows, :]).astype(BF16)
            return carry

        lax.fori_loop(0, 8, finish, 0, unroll=2)
        rows = pl.ds(part * 256, 256)
        outs.append(start(weight.at[rows], weight_hbm.at[rows], out_sems.at[3 + part]))

    params = vectors[...]
    first_new, second_new, u = step_of(
        grad_vectors * factor, vec_first[...], vec_second[...], params, 0.0
    )
    trust = jnp.sqrt(jnp.sum(params * params, axis=1, keepdims=True)) / jnp.sqrt(
        jnp.sum(u * u, axis=1, keepdims=True) + 1e-06
    )
    vec_out[...] = params - learn_rate * trust * u
    vec_first_out[...] = first_new
    vec_second_out[...] = second_new
    for copy in outs:
        copy.wait()


def on_device(
    context,
    residual_in,
    cotangent,
    weight,
    master,
    moment_first,
    moment_second,
    out_bias,
    ln_gain,
    ln_shift,
    vector_first,
    vector_second,
):
    d_resid, send, keep, packed = backward(
        context,
        residual_in,
        cotangent,
        weight,
        out_bias.reshape(1, D),
        ln_gain.reshape(1, D),
        master,
        moment_first,
        moment_second,
    )
    got = other_core(send)
    (packed,) = call(
        pass_kernel,
        [((2, 3, 128, D), BF16)],
        (packed,),
        specs=[ANY],
        out_specs=[ANY],
        input_output_aliases={0: 0},
        cost=pl.CostEstimate(flops=4 * D**3, bytes_accessed=0, transcendentals=0),
        limit=58,
    )
    near = next_shard(packed)
    d_context, token = context_grad(d_resid, weight)

    (pieces,) = call(core_kernel, [((16, PIECE, 128), BF16)], (keep, got), limit=8)
    pieces = exchange_plane(pieces)
    (pieces,) = call(
        functools.partial(sum_kernel, 16, 4),
        [((4, PIECE, 128), BF16)],
        (pieces,),
        limit=8,
    )
    half_at = lax.axis_index("c") + token[0, 0].astype(jnp.int32)
    far = next_shard(lax.dynamic_index_in_dim(near, half_at, keepdims=False))
    pieces = exchange_z(pieces)
    (pieces,) = call(
        functools.partial(sum_kernel, 4, 16),
        [((16, PIECE, 128), BF16)],
        (pieces,),
        limit=8,
    )
    near_other, far_other = other_core(near), other_core(far)
    pieces = exchange_plane(pieces)
    shard = ((256, D), F32)
    rows = ((3, D), F32)
    *state, weight_sq = call(
        stage_kernel,
        [((D, D), BF16)] * 3 + [((8, D), F32)],
        (near, near_other, far, far_other, master, moment_first, moment_second),
        cost=pl.CostEstimate(flops=D**3, bytes_accessed=16 * MIB, transcendentals=0),
        limit=53,
    )
    (mine,) = call(
        half_kernel,
        [((528, D), BF16)],
        (pieces, weight_sq),
        specs=[VMEM, ANY],
        limit=8,
    )
    others = other_core(mine)
    (token,) = call(
        token_kernel,
        [((8, 128), F32)],
        (mine,),
        specs=[ANY],
        cost=pl.CostEstimate(flops=30 * D**3, bytes_accessed=0, transcendentals=0),
        limit=16,
    )

    vectors = jnp.stack([out_bias, ln_gain, ln_shift])
    outs = call(
        lamb_kernel,
        [((D, D), BF16), shard, shard, shard, rows, rows, rows],
        (
            mine,
            others,
            *state,
            master,
            moment_first,
            moment_second,
            weight_sq,
            vectors,
            vector_first,
            vector_second,
            token,
        ),
        out_specs=[HBM] * 4 + [VMEM] * 3,
        scratch=[
            pltpu.VMEM((D, D), F32),
            pltpu.VMEM((256, D), F32),
            pltpu.VMEM((2, 8, D), F32),
            pltpu.VMEM((3, 256, D), F32),
            pltpu.VMEM((D, D), BF16),
            DMA((7,)),
        ],
        limit=28,
    )
    return (d_context, d_resid, *outs)


def solution(mesh):
    mesh = Mesh(mesh.devices.reshape(4, 4, 2, 4), AXES)
    tokens, copied, shard = P(AXES, None), P(), P("z", None)
    return jax.shard_map(
        on_device,
        mesh=mesh,
        in_specs=(tokens,) * 3 + (copied,) + (shard,) * 3 + (copied,) * 5,
        out_specs=(tokens, tokens, copied) + (shard,) * 3 + (copied,) * 3,
        check_vma=False,
    )
```
